128 devices in a mesh: rows: 8 (over z_lo, x), cols: 16 (over y, z_hi, core).
Axes of the slice: x: 4, y: 4, z: 4 (z_hi: 2, z_lo: 2; z = z_hi * 2 + z_lo), core: 2. Of those that a mesh axis runs over, the one named last changes fastest.
Arguments:
- model: bfloat16 [256, 512, 512], P(('rows', 'cols')), may hold values from -6 to 6
- dirty: bfloat16 [256, 512, 512], P(('rows', 'cols')), may hold values from -6 to 6
- psf: bfloat16 [256, 256, 256], P(('rows', 'cols')), may hold values from -0.0234375 to 0.0234375
- step_size: float32 [256], P(('rows', 'cols')), may hold values from 0.2 to 1
- gain: float32 [256], replicated, may hold values from 0.1 to 1.9
- w_in: bfloat16 [256, 256], replicated, may hold values from -0.375 to 0.375
- b_in: float32 [256], replicated, may hold values from -3 to 3
- w_out: bfloat16 [256, 256], replicated, may hold values from -0.375 to 0.375
- kernel: float32 [3, 3, 256], replicated, may hold values from -2 to 2
Outputs:
- updated_model: bfloat16 [256, 512, 512], P(('rows', 'cols'))
The draws below stay inside these ranges and needn't reach their ends.
All inputs are finite; a program needn't handle non-finite values.
Results may differ from the reference program's by a relative error of at most 0.0095.
Values may be sent and summed in bfloat16 or wider, within the bound.
A program may use at most 64 MiB of HBM per device.

```python
import math
import jax
import jax.numpy as jnp
from jax import lax

IMG = 512
FFT = 1024
PSF = 256
HIDDEN_SIZE = 256
CHANNELS = 256


def block_scale(stream_key, extent, pieces, low, top_value):
    def one(position, shards_of):
        steps = jax.random.uniform(jax.random.fold_in(jax.random.fold_in(stream_key, 6), position), (shards_of,), jnp.float32, low / len(pieces), top_value / len(pieces))
        return jnp.repeat(jnp.exp(steps), extent[position] // shards_of).reshape((-1,) + (1,) * (len(extent) - position - 1))

    level = one(*pieces[0])
    for cut in pieces[1:]:
        level = level * one(*cut)
    return level


def bell_draw(own_key, dims, scale, bound, cuts=(), held_as=jnp.bfloat16):
    level = block_scale(own_key, dims, cuts, -0.22, 0.18) if cuts else 1.0
    entries = jax.random.normal(own_key, dims, jnp.float32) * scale * level
    return jnp.minimum(jnp.maximum(entries, -bound), bound).astype(held_as)


def setup_inputs(seed: int = 0) -> dict:
    arg_keys = jax.random.split(jax.random.key(seed), 10)
    return {
        "model": bell_draw(arg_keys[0], (CHANNELS, IMG, IMG), 1.0, 6.0, ((0, 128),)),
        "dirty": bell_draw(arg_keys[1], (CHANNELS, IMG, IMG), 1.0, 6.0, ((0, 128),)),
        "psf": bell_draw(arg_keys[2], (CHANNELS, PSF, PSF), (PSF * PSF) ** -0.5, 0.0234375, ((0, 128),)),
        "step_size": jnp.clip(jnp.exp(math.log(1.0) - 1.609438 * jax.random.uniform(arg_keys[3], (CHANNELS,), jnp.float32) ** block_scale(arg_keys[3], (CHANNELS,), ((0, 128),), -0.2, 0.2)), 0.2, 1.0),
        "gain": jnp.clip(1.0 + 0.18 * jax.random.normal(arg_keys[4], (CHANNELS,), jnp.float32), 0.1, 1.9),
        "w_in": bell_draw(arg_keys[5], (CHANNELS, HIDDEN_SIZE), CHANNELS ** -0.5, 0.375),
        "b_in": bell_draw(arg_keys[6], (HIDDEN_SIZE,), 0.5, 3.0, (), jnp.float32),
        "w_out": bell_draw(arg_keys[7], (HIDDEN_SIZE, CHANNELS), HIDDEN_SIZE ** -0.5, 0.375),
        "kernel": bell_draw(arg_keys[8], (3, 3, CHANNELS), 9 ** -0.5, 2.0, (), jnp.float32),
    }


def tables(length, count, offset):
    freq = jnp.arange(length, dtype=jnp.int32)[:, None]
    place = jnp.arange(count, dtype=jnp.int32)[None, :] + offset
    phase = (freq * place % length).astype(jnp.float32) * (2.0 * math.pi / length)
    return (jnp.cos(phase).astype(jnp.bfloat16), jnp.sin(phase).astype(jnp.bfloat16))

def spectrum(plane, cos_t, sin_t):
    real_a = jnp.dot(cos_t, plane, preferred_element_type=jnp.float32).astype(jnp.bfloat16)
    imag_a = (-jnp.dot(sin_t, plane, preferred_element_type=jnp.float32)).astype(jnp.bfloat16)
    real_s = jnp.dot(real_a, cos_t.T, preferred_element_type=jnp.float32) + jnp.dot(imag_a, sin_t.T, preferred_element_type=jnp.float32)
    imag_s = jnp.dot(imag_a, cos_t.T, preferred_element_type=jnp.float32) - jnp.dot(real_a, sin_t.T, preferred_element_type=jnp.float32)
    return (real_s, imag_s)

def convolve(plane, spread_fn, image_tabs, psf_tabs, window_tabs, length):
    real_x, imag_x = spectrum(plane, image_tabs[0], image_tabs[1])
    real_q, imag_q = spectrum(spread_fn, psf_tabs[0], psf_tabs[1])
    factor = 1.0 / (length * length)
    real_p = ((real_x * real_q - imag_x * imag_q) * factor).astype(jnp.bfloat16)
    imag_p = ((real_x * imag_q + imag_x * real_q) * factor).astype(jnp.bfloat16)
    cos_w, sin_w = window_tabs
    real_b = (jnp.dot(real_p, cos_w, preferred_element_type=jnp.float32) - jnp.dot(imag_p, sin_w, preferred_element_type=jnp.float32)).astype(jnp.bfloat16)
    imag_b = (jnp.dot(real_p, sin_w, preferred_element_type=jnp.float32) + jnp.dot(imag_p, cos_w, preferred_element_type=jnp.float32)).astype(jnp.bfloat16)
    return jnp.dot(cos_w.T, real_b, preferred_element_type=jnp.float32) - jnp.dot(sin_w.T, imag_b, preferred_element_type=jnp.float32)

def prior_mix(pixels, gain, w_in, b_in, w_out):
    values = pixels.astype(jnp.float32)
    power = lax.optimization_barrier(jnp.mean(values * values, axis=0, keepdims=True))
    normed = (values / jnp.sqrt(power + 1e-06) * gain[:, None]).astype(jnp.bfloat16)
    inner = jnp.dot(w_in.T, normed, preferred_element_type=jnp.float32) + b_in[:, None]
    hidden = jax.nn.gelu(inner, approximate=True).astype(jnp.bfloat16)
    return jnp.dot(w_out.T, hidden, preferred_element_type=jnp.float32).astype(jnp.bfloat16)

def spread(padded, kernel, height, width):
    total = jnp.zeros((padded.shape[0], height, width), jnp.float32)
    for row_tap in range(3):
        for col_tap in range(3):
            total = total + kernel[row_tap, col_tap][:, None, None] * padded[:, row_tap:row_tap + height, col_tap:col_tap + width].astype(jnp.float32)
    return total

def reference(model, dirty, psf, step_size, gain, w_in, b_in, w_out, kernel):
    image_tabs = tables(FFT, IMG, 0)
    psf_tabs = tables(FFT, PSF, 0)
    window_tabs = tables(FFT, IMG, PSF // 2)

    def one_channel(items):
        plane, dirty_plane, psf_plane, rate = items
        blurred = convolve(plane, psf_plane, image_tabs, psf_tabs, window_tabs, FFT)
        return (plane.astype(jnp.float32) + rate * (dirty_plane.astype(jnp.float32) - blurred)).astype(jnp.bfloat16)
    stepped = lax.map(one_channel, (model, dirty, psf, step_size))
    mixed = prior_mix(stepped.reshape(CHANNELS, IMG * IMG), gain, w_in, b_in, w_out).reshape(CHANNELS, IMG, IMG)
    padded = jnp.pad(mixed, ((0, 0), (1, 1), (1, 1)))
    return (stepped.astype(jnp.float32) + spread(padded, kernel, IMG, IMG)).astype(jnp.bfloat16)
```

```python
import functools
import math

import jax
import jax.numpy as jnp
import ml_dtypes
import numpy as np
from jax import lax
from jax.experimental import pallas as pl
from jax.experimental.pallas import tpu as pltpu
from jax.sharding import PartitionSpec as P

BF16 = jnp.bfloat16
F32 = jnp.float32
IMG = 512
PSF = 256
LEN = IMG + PSF // 2
HALF = LEN // 2
TILE = 16
LANES = 128
STEP_COLS = 128


def angle(freq, place):
    turns = (2.0 * freq[:, None]) * place[None, :]
    return np.mod(turns, 2 * LEN) * (math.pi / LEN)


def make_tables():
    odd = np.arange(HALF) + 0.5
    even = np.arange(LEN).astype(np.float64)
    place = np.arange(IMG).astype(np.float64)
    window = place + PSF // 2
    first = angle(odd, place)
    rows_in = np.concatenate([np.cos(first), -np.sin(first)], axis=0)
    second = angle(even, place).T
    parts = []
    for start in range(0, LEN, STEP_COLS):
        cos = np.cos(second[:, start : start + STEP_COLS])
        sin = np.sin(second[:, start : start + STEP_COLS])
        parts.append(
            np.concatenate(
                [np.concatenate([cos, -sin], axis=1), np.concatenate([sin, cos], axis=1)], axis=0
            )
        )
    cols_in = np.stack(parts)
    back = angle(even, window)
    parts = []
    for start in range(0, LEN, STEP_COLS):
        cos = np.cos(back[start : start + STEP_COLS])
        sin = np.sin(back[start : start + STEP_COLS])
        parts.append(np.concatenate([cos, sin], axis=1))
        parts.append(np.concatenate([-sin, cos], axis=1))
    cols_out = np.concatenate(parts, axis=0)
    cols_out = np.stack(np.split(cols_out, 4, axis=1))
    last = angle(odd, window).T
    rows_out = np.concatenate([2 * np.cos(last), -2 * np.sin(last)], axis=1)
    swap = np.zeros((256, 256))
    index = np.arange(256)
    swap[index, (index % 16) * 16 + index // 16] = 1
    return [x.astype(ml_dtypes.bfloat16) for x in (rows_in, cols_in, cols_out, rows_out, swap)]


def dot(a, b):
    return jnp.dot(a, b, preferred_element_type=F32)


def deconvolve(plane, dirty, psf, rate, rows_in, cols_in, cols_out, rows_out, stepped, work):
    image, point, prod, back = work
    count = LEN // STEP_COLS
    low = dot(rows_in[...], plane[...]).astype(BF16)
    image[:, :IMG] = low[:HALF]
    image[:, IMG:] = low[HALF:]
    low = dot(rows_in[:, :PSF], psf[...]).astype(BF16)
    point[:, :PSF] = low[:HALF]
    point[:, PSF:] = low[HALF:]

    def columns(step, carry):
        tab = cols_in.at[step]
        x = dot(image[...], tab[...])
        q = dot(point[:, :PSF], tab[:PSF]) + dot(point[:, PSF:], tab[IMG : IMG + PSF])
        x = x * (1.0 / (LEN * LEN))
        real_x, imag_x = x[:, :STEP_COLS], x[:, STEP_COLS:]
        real_q, imag_q = q[:, :STEP_COLS], q[:, STEP_COLS:]
        prod[step, :, :STEP_COLS] = (real_x * real_q - imag_x * imag_q).astype(BF16)
        prod[step, :, STEP_COLS:] = (real_x * imag_q + imag_x * real_q).astype(BF16)
        return carry

    lax.fori_loop(0, count, columns, 0)
    for part in range(4):
        tab = cols_out.at[part]
        total = dot(prod[0], tab[: 2 * STEP_COLS])
        for step in range(1, count):
            total += dot(prod[step], tab[2 * STEP_COLS * step : 2 * STEP_COLS * (step + 1)])
        row, col = divmod(part, 2)
        back[row * HALF : (row + 1) * HALF, col * 256 : (col + 1) * 256] = total.astype(BF16)

    def rows(step, carry):
        at = pl.ds(pl.multiple_of(step * 128, 128), 128)
        blurred = dot(rows_out[at, :], back[...])
        held = plane[at, :].astype(F32)
        stepped[at, :] = (held + rate * (dirty[at, :].astype(F32) - blurred)).astype(BF16)
        return carry

    lax.fori_loop(0, IMG // 128, rows, 0)


def mix(tiles, gain, w_in, b_in, w_out, swap, mixed, work):
    normed, turned = work

    def power_of(group, total):
        at = pl.ds(pl.multiple_of(group * 256, 256), 256)
        v = tiles[at, :].astype(F32)
        v = v * v
        return total + jnp.sum(v.reshape(16, TILE, LANES), axis=0)

    power = lax.fori_loop(0, 16, power_of, jnp.zeros((TILE, LANES), F32))
    scale = lax.rsqrt(power * (1.0 / 256) + 1e-06)

    def turn(pair, carry):
        for side in range(2):
            group = pair * 2 + side
            for k in range(16):
                channel = group * 16 + k
                v = tiles[pl.ds(pl.multiple_of(channel * TILE, TILE), TILE), :].astype(F32)
                normed[k * 16 : (k + 1) * 16, side * LANES : (side + 1) * LANES] = (
                    v * scale * gain[channel]
                ).astype(BF16)
        moved = dot(swap[...], normed[...]).astype(BF16)
        for side in range(2):
            at = pl.ds(pl.multiple_of((pair * 2 + side) * 16, 16), 16)
            for r in range(TILE):
                turned[r // 2, at, (r % 2) * LANES : (r % 2 + 1) * LANES] = moved[
                    r * 16 : (r + 1) * 16, side * LANES : (side + 1) * LANES
                ]
        return carry

    lax.fori_loop(0, 8, turn, 0)
    w_in_t = w_in[...].astype(F32).T.astype(BF16)
    w_out_t = w_out[...].astype(F32).T.astype(BF16)
    bias = b_in[...]

    def layers(pair, carry):
        inner = dot(w_in_t, turned[pair]) + bias
        hidden = jax.nn.gelu(inner, approximate=True).astype(BF16)
        turned[pair] = dot(w_out_t, hidden).astype(BF16)
        return carry

    lax.fori_loop(0, TILE // 2, layers, 0)

    def turn_back(pair, carry):
        for side in range(2):
            at = pl.ds(pl.multiple_of((pair * 2 + side) * 16, 16), 16)
            for r in range(TILE):
                normed[r * 16 : (r + 1) * 16, side * LANES : (side + 1) * LANES] = turned[
                    r // 2, at, (r % 2) * LANES : (r % 2 + 1) * LANES
                ]
        moved = dot(swap[...], normed[...]).astype(BF16)
        for side in range(2):
            at = pl.ds(pl.multiple_of((pair * 2 + side) * 256, 256), 256)
            mixed[at, :] = moved[:, side * LANES : (side + 1) * LANES]
        return carry

    lax.fori_loop(0, 8, turn_back, 0)


def filter_plane(mixed, stepped, taps, out, wide):
    zero = jnp.zeros((8, IMG), F32)
    wide[:8] = zero
    wide[8 + IMG :] = zero

    def widen(step, carry):
        at = pl.multiple_of(step * 64, 64)
        wide[pl.ds(at + 8, 64), :] = mixed[pl.ds(at, 64), :].astype(F32)
        return carry

    lax.fori_loop(0, IMG // 64, widen, 0)
    rows = 32
    lane = lax.broadcasted_iota(jnp.int32, (rows, IMG), 1)

    def block(step, carry):
        at = pl.multiple_of(step * rows, rows)
        span = wide[pl.ds(at, rows + 16), :]
        lines = [span[7 + a : 7 + a + rows] for a in range(3)]
        sums = [sum(taps(a, b) * lines[a] for a in range(3)) for b in range(3)]
        left = jnp.where(lane == 0, 0.0, pltpu.roll(sums[0], 1, 1))
        right = jnp.where(lane == IMG - 1, 0.0, pltpu.roll(sums[2], IMG - 1, 1))
        total = stepped[pl.ds(at, rows), :].astype(F32) + (sums[1] + (left + right))
        out[pl.ds(at, rows), :] = total.astype(BF16)
        return carry

    lax.fori_loop(0, IMG // rows, block, 0)


def step_kernel(rate, model, dirty, psf, rows_in, cols_in, cols_out, rows_out, out, *work):
    for channel in range(2):
        deconvolve(
            model.at[channel], dirty.at[channel], psf.at[channel], rate[channel],
            rows_in, cols_in, cols_out, rows_out, out.at[channel], work,
        )


def mix_kernel(gain, tiles, w_in, b_in, w_out, swap, out, *work):
    mix(tiles, gain, w_in, b_in, w_out, swap, out, work)


def filter_kernel(taps, mixed, stepped, out, wide):
    for channel in range(2):
        filter_plane(
            mixed.at[channel], stepped.at[channel],
            lambda a, b: taps[channel * 9 + a * 3 + b], out.at[channel], wide,
        )


def local(model, dirty, psf, step_size, gain, w_in, b_in, w_out, kernel):
    rows_in, cols_in, cols_out, rows_out, swap = make_tables()
    smem = pl.BlockSpec(memory_space=pltpu.SMEM)
    vmem = pl.BlockSpec(memory_space=pltpu.VMEM)
    params = pltpu.CompilerParams(vmem_limit_bytes=56 << 20)
    stepped = pl.pallas_call(
        step_kernel,
        out_shape=jax.ShapeDtypeStruct((2, IMG, IMG), BF16),
        in_specs=[smem] + [vmem] * 7,
        out_specs=vmem,
        scratch_shapes=[
            pltpu.VMEM((HALF, 2 * IMG), BF16),
            pltpu.VMEM((HALF, 2 * PSF), BF16),
            pltpu.VMEM((LEN // STEP_COLS, HALF, 2 * STEP_COLS), BF16),
            pltpu.VMEM((LEN, IMG), BF16),
        ],
        compiler_params=params,
    )(step_size, model, dirty, psf, rows_in, cols_in, cols_out, rows_out)

    blocks = stepped.reshape(2, 32, TILE, 4, LANES).transpose(1, 3, 0, 2, 4)
    blocks = blocks.reshape(128, 2, TILE, LANES)
    tiles = lax.all_to_all(blocks, ("rows", "cols"), split_axis=0, concat_axis=0, tiled=True)
    mixed = pl.pallas_call(
        mix_kernel,
        out_shape=jax.ShapeDtypeStruct((256 * TILE, LANES), BF16),
        in_specs=[smem] + [vmem] * 5,
        out_specs=vmem,
        scratch_shapes=[pltpu.VMEM((256, 256), BF16), pltpu.VMEM((TILE // 2, 256, 256), BF16)],
        compiler_params=params,
    )(gain, tiles.reshape(256 * TILE, LANES), w_in, b_in[:, None], w_out, swap)
    back = lax.all_to_all(
        mixed.reshape(128, 2, TILE, LANES), ("rows", "cols"), split_axis=0, concat_axis=0, tiled=True
    )
    planes = back.reshape(32, 4, 2, TILE, LANES).transpose(2, 0, 3, 1, 4).reshape(2, IMG, IMG)
    me = lax.axis_index(("rows", "cols"))
    taps = lax.dynamic_slice_in_dim(kernel.reshape(9, 256), 2 * me, 2, axis=1).T.reshape(18)
    return pl.pallas_call(
        filter_kernel,
        out_shape=jax.ShapeDtypeStruct((2, IMG, IMG), BF16),
        in_specs=[smem] + [vmem] * 2,
        out_specs=vmem,
        scratch_shapes=[pltpu.VMEM((IMG + 16, IMG), F32)],
        compiler_params=params,
    )(taps, planes, stepped)


def solution(mesh):
    split = P(("rows", "cols"), None, None)
    return jax.shard_map(
        local,
        mesh=mesh,
        in_specs=(split, split, split, P(("rows", "cols")), P(), P(), P(), P(), P()),
        out_specs=split,
        check_vma=False,
    )
```

```python
import math

import jax
import jax.numpy as jnp
import ml_dtypes
import numpy as np
from jax import lax
from jax.experimental import pallas as pl
from jax.experimental.pallas import tpu as pltpu
from jax.sharding import PartitionSpec as P

BF16 = jnp.bfloat16
F32 = jnp.float32
MESH = pl.DeviceIdType.MESH
IMG = 512
PSF = 256
LEN = IMG + PSF // 2
HALF = LEN // 2
TILE = 16
LANES = 128
CHIPS = 64
STEP_COLS = 128


def angle(freq, place):
    turns = (2.0 * freq[:, None]) * place[None, :]
    return np.mod(turns, 2 * LEN) * (math.pi / LEN)


def make_tables():
    odd = np.arange(HALF) + 0.5
    even = np.arange(LEN).astype(np.float64)
    place = np.arange(IMG).astype(np.float64)
    window = place + PSF // 2
    first = angle(odd, place)
    rows_in = np.concatenate([np.cos(first), -np.sin(first)], axis=0)
    second = angle(even, place).T
    parts = []
    for start in range(0, LEN, STEP_COLS):
        cos = np.cos(second[:, start : start + STEP_COLS])
        sin = np.sin(second[:, start : start + STEP_COLS])
        parts.append(
            np.concatenate(
                [np.concatenate([cos, -sin], axis=1), np.concatenate([sin, cos], axis=1)], axis=0
            )
        )
    cols_in = np.stack(parts)
    back = angle(even, window)
    parts = []
    for start in range(0, LEN, STEP_COLS):
        cos = np.cos(back[start : start + STEP_COLS])
        sin = np.sin(back[start : start + STEP_COLS])
        parts.append(np.concatenate([cos, sin], axis=1))
        parts.append(np.concatenate([-sin, cos], axis=1))
    cols_out = np.concatenate(parts, axis=0)
    cols_out = np.stack(np.split(cols_out, 4, axis=1))
    last = angle(odd, window).T
    rows_out = np.concatenate([2 * np.cos(last), -2 * np.sin(last)], axis=1)
    swap = np.zeros((256, 256))
    index = np.arange(256)
    swap[index, (index % 16) * 16 + index // 16] = 1
    order = np.zeros((256, 256))
    order[index, (index % 2) * 128 + index // 2] = 1
    tables = (rows_in, cols_in, cols_out, rows_out, swap, order)
    return [x.astype(ml_dtypes.bfloat16) for x in tables]


def dot(a, b):
    return jnp.dot(a, b, preferred_element_type=F32)


def copy_here(src, dst, sem):
    return pltpu.make_async_copy(src, dst, sem)


def first_axis(plane, psf, rows_in, image, point):
    low = dot(rows_in[...], plane[...]).astype(BF16)
    image[:, :IMG] = low[:HALF]
    image[:, IMG:] = low[HALF:]
    low = dot(rows_in[:, :PSF], psf[...]).astype(BF16)
    point[:, :PSF] = low[:HALF]
    point[:, PSF:] = low[HALF:]


def second_axis(cols_in, image, point, prod):
    def columns(step, carry):
        tab = cols_in.at[step]
        x = dot(image[...], tab[...])
        q = dot(point[:, :PSF], tab[:PSF]) + dot(point[:, PSF:], tab[IMG : IMG + PSF])
        x = x * (1.0 / (LEN * LEN))
        real_x, imag_x = x[:, :STEP_COLS], x[:, STEP_COLS:]
        real_q, imag_q = q[:, :STEP_COLS], q[:, STEP_COLS:]
        prod[step, :, :STEP_COLS] = (real_x * real_q - imag_x * imag_q).astype(BF16)
        prod[step, :, STEP_COLS:] = (real_x * imag_q + imag_x * real_q).astype(BF16)
        return carry

    lax.fori_loop(0, LEN // STEP_COLS, columns, 0)


def second_axis_back(cols_out, prod, back):
    for part in range(4):
        tab = cols_out.at[part]
        total = dot(prod[0], tab[: 2 * STEP_COLS])
        for step in range(1, LEN // STEP_COLS):
            total += dot(prod[step], tab[2 * STEP_COLS * step : 2 * STEP_COLS * (step + 1)])
        row, col = divmod(part, 2)
        back[row * HALF : (row + 1) * HALF, col * 256 : (col + 1) * 256] = total.astype(BF16)


def filter_plane(mixed, stepped, taps, out, wide):
    zero = jnp.zeros((8, IMG), F32)
    wide[:8] = zero
    wide[8 + IMG :] = zero

    def widen(step, carry):
        at = pl.multiple_of(step * 64, 64)
        wide[pl.ds(at + 8, 64), :] = mixed[pl.ds(at, 64), :].astype(F32)
        return carry

    lax.fori_loop(0, IMG // 64, widen, 0)
    rows = 32
    lane = lax.broadcasted_iota(jnp.int32, (rows, IMG), 1)

    def block(step, carry):
        at = pl.multiple_of(step * rows, rows)
        span = wide[pl.ds(at, rows + 16), :]
        lines = [span[7 + a : 7 + a + rows] for a in range(3)]
        sums = [sum(taps(a, b) * lines[a] for a in range(3)) for b in range(3)]
        left = jnp.where(lane == 0, 0.0, pltpu.roll(sums[0], 1, 1))
        right = jnp.where(lane == IMG - 1, 0.0, pltpu.roll(sums[2], IMG - 1, 1))
        total = stepped[pl.ds(at, rows), :].astype(F32) + (sums[1] + (left + right))
        out[pl.ds(at, rows), :] = total.astype(BF16)
        return carry

    lax.fori_loop(0, IMG // rows, block, 0)


def whole(
    rate, taps, model_h, dirty_h, psf_h, rows_in_h, cols_in_h, cols_out_h, rows_out_h,
    swap, order, gain, w_in, b_in, w_out, out_h,
    model, dirty, psf, rows_in, cols_in, cols_out, rows_out,
    image, point, prod, back, stepped, halves, parcel, tiles, turned, inner, scale,
    mixed, returned, planes, out, wide,
    load_sem, out_sem, pair_send, pair_recv, go_send, go_recv, ret_send, ret_recv, fin_send, fin_recv,
):
    row_at, col_at = lax.axis_index("rows"), lax.axis_index("cols")
    chip = row_at * 8 + col_at // 2
    core = col_at % 2
    sibling = {"rows": row_at, "cols": col_at + 1 - 2 * core}

    def at_chip(other):
        return {"rows": other // 8, "cols": (other % 8) * 2 + core}

    loads = []
    for src, dst in (
        (rows_in_h, rows_in),
        (model_h.at[0], model.at[0]),
        (psf_h, psf),
        (cols_in_h, cols_in),
        (cols_out_h, cols_out),
        (rows_out_h, rows_out),
        (dirty_h, dirty),
        (model_h.at[1], model.at[1]),
    ):
        copy = copy_here(src, dst, load_sem.at[len(loads)])
        copy.start()
        loads.append(copy)

    barrier = pltpu.get_barrier_semaphore()
    pl.semaphore_signal(barrier, inc=1, device_id=sibling, device_id_type=MESH)

    def greet(k, carry):
        pl.semaphore_signal(barrier, inc=1, device_id=at_chip(chip ^ k), device_id_type=MESH)
        return carry

    lax.fori_loop(1, CHIPS, greet, 0)

    def last_axis(channel):
        def rows(step, carry):
            at = pl.ds(pl.multiple_of(step * 128, 128), 128)
            blurred = dot(rows_out[at, :], back[...])
            held = model[channel, at, :].astype(F32)
            ahead = held + rate[channel] * (dirty[channel, at, :].astype(F32) - blurred)
            ahead = ahead.astype(BF16)
            stepped[channel, at, :] = ahead
            mine = jnp.where(core == 0, ahead[:, :256], ahead[:, 256:])
            other = jnp.where(core == 0, ahead[:, 256:], ahead[:, :256])
            halves[channel, core, at, :] = mine
            parcel[channel, at, :] = other
            return carry

        lax.fori_loop(0, IMG // 128, rows, 0)

    def pair_copy(channel):
        return pltpu.make_async_remote_copy(
            src_ref=parcel.at[channel],
            dst_ref=halves.at[channel, core],
            send_sem=pair_send.at[channel],
            recv_sem=pair_recv.at[channel],
            device_id=sibling,
            device_id_type=MESH,
        )

    def tile_of(planes_ref, other):
        at = pl.ds(pl.multiple_of((other // 2) * TILE, TILE), TILE)
        return planes_ref.at[:, at, pl.ds(pl.multiple_of((other % 2) * LANES, LANES), LANES)]

    def send_tiles(channel):
        def send(k, carry):
            other = chip ^ k
            pltpu.make_async_remote_copy(
                src_ref=tile_of(halves.at[channel], other),
                dst_ref=tiles.at[channel, pl.ds(chip * 2, 2)],
                send_sem=go_send.at[channel],
                recv_sem=go_recv.at[channel],
                device_id=at_chip(other),
                device_id_type=MESH,
            ).start()
            return carry

        lax.fori_loop(1, CHIPS, send, 0)
        copy_here(
            tile_of(halves.at[channel], chip),
            tiles.at[channel, pl.ds(chip * 2, 2)],
            go_recv.at[channel],
        ).start()

    def return_tiles(channel):
        def send(k, carry):
            other = chip ^ k
            pltpu.make_async_remote_copy(
                src_ref=mixed.at[channel, pl.ds(other * 2, 2)],
                dst_ref=tile_of(returned.at[channel], chip),
                send_sem=ret_send.at[channel],
                recv_sem=ret_recv.at[channel],
                device_id=at_chip(other),
                device_id_type=MESH,
            ).start()
            return carry

        lax.fori_loop(1, CHIPS, send, 0)
        copy_here(
            mixed.at[channel, pl.ds(chip * 2, 2)],
            tile_of(returned.at[channel], chip),
            ret_recv.at[channel],
        ).start()

    def half_at(which):
        return pl.ds(pl.multiple_of(which * 256, 256), 256)

    def final_copy(channel):
        return pltpu.make_async_remote_copy(
            src_ref=returned.at[channel, 1 - core],
            dst_ref=planes.at[channel, :, half_at(core)],
            send_sem=fin_send.at[channel],
            recv_sem=fin_recv.at[channel],
            device_id=sibling,
            device_id_type=MESH,
        )

    for load in loads[:3]:
        load.wait()
    first_axis(model.at[0], psf.at[0], rows_in, image, point)
    loads[3].wait()
    second_axis(cols_in, image, point, prod)
    loads[4].wait()
    second_axis_back(cols_out, prod, back)
    loads[5].wait()
    loads[6].wait()
    last_axis(0)
    pl.semaphore_wait(barrier, CHIPS)
    pair_copy(0).start()
    loads[7].wait()
    first_axis(model.at[1], psf.at[1], rows_in, image, point)
    pair_copy(0).wait_recv()
    send_tiles(0)
    second_axis(cols_in, image, point, prod)
    second_axis_back(cols_out, prod, back)
    last_axis(1)
    pair_copy(1).start()

    w_in_t = (w_in[...].astype(F32).T * gain[...]).astype(BF16)
    w_in_t = dot(w_in_t, order[...]).astype(BF16)
    w_out_t = dot(w_out[...], order[...]).T.astype(BF16)
    bias = jnp.broadcast_to(b_in[...], (LANES, 256)).T
    bias = jnp.concatenate([bias, bias], axis=1)

    pair_copy(1).wait_recv()
    send_tiles(1)

    def power_of(channel, total):
        def add(group, total):
            v = tiles[channel, pl.ds(pl.multiple_of(group * 16, 16), 16)].astype(F32)
            return total + jnp.sum(v * v, axis=0)

        return lax.fori_loop(0, 8, add, total)

    def turn(channel):
        def pairs(pair, carry):
            sides = [
                tiles[channel, pl.ds(pl.multiple_of(pair * 32 + side * 16, 16), 16)].reshape(256, LANES)
                for side in range(2)
            ]
            moved = dot(swap[...], jnp.concatenate(sides, axis=1)).astype(BF16)
            for side in range(2):
                at = pl.ds(pl.multiple_of(pair * 32 + side * 16, 16), 16)
                for r in range(TILE):
                    turned[channel, r // 2, at, (r % 2) * LANES : (r % 2 + 1) * LANES] = moved[
                        r * 16 : (r + 1) * 16, side * LANES : (side + 1) * LANES
                    ]
            return carry

        lax.fori_loop(0, 4, pairs, 0)

    def turn_back(channel):
        def pairs(pair, carry):
            sides = []
            for side in range(2):
                at = pl.ds(pl.multiple_of(pair * 32 + side * 16, 16), 16)
                lines = [
                    turned[channel, r // 2, at, (r % 2) * LANES : (r % 2 + 1) * LANES]
                    for r in range(TILE)
                ]
                sides.append(jnp.concatenate(lines, axis=0))
            moved = dot(swap[...], jnp.concatenate(sides, axis=1)).astype(BF16)
            for side in range(2):
                at = pl.ds(pl.multiple_of(pair * 32 + side * 16, 16), 16)
                mixed[channel, at] = moved[:, side * LANES : (side + 1) * LANES].reshape(16, TILE, LANES)
            return carry

        lax.fori_loop(0, 4, pairs, 0)

    copy_here(tiles.at[0], tiles.at[0], go_recv.at[0]).wait()
    power = power_of(0, jnp.zeros((TILE, LANES), F32))
    turn(0)

    def layer_part(pair, carry):
        inner[pair] = dot(w_in_t[:, :128], turned[0, pair])
        return carry

    lax.fori_loop(0, TILE // 2, layer_part, 0)
    copy_here(tiles.at[1], tiles.at[1], go_recv.at[1]).wait()
    power = power_of(1, power)
    scale[...] = lax.rsqrt(power * (1.0 / 256) + 1e-06)
    turn(1)

    def layers(pair, carry):
        factor = jnp.concatenate([scale[pl.ds(2 * pair, 1), :], scale[pl.ds(2 * pair + 1, 1), :]], axis=1)
        total = inner[pair] + dot(w_in_t[:, 128:], turned[1, pair])
        hidden = jax.nn.gelu(total * factor + bias, approximate=True).astype(BF16)
        result = dot(w_out_t, hidden).astype(BF16)
        turned[0, pair] = result[:128]
        turned[1, pair] = result[128:]
        return carry

    lax.fori_loop(0, TILE // 2, layers, 0)
    for channel in range(2):
        turn_back(channel)
        return_tiles(channel)

    for channel in range(2):
        copy_here(returned.at[channel], returned.at[channel], ret_recv.at[channel]).wait()
        final_copy(channel).start()
        planes[channel, :, half_at(core)] = returned[channel, core]
        final_copy(channel).wait_recv()
        filter_plane(
            planes.at[channel], stepped.at[channel],
            lambda a, b: taps[a, b, (chip * 2 + core) * 2 + channel], out.at[channel], wide,
        )
        copy_here(out.at[channel], out_h.at[channel], out_sem.at[channel]).start()
    for channel in range(2):
        pair_copy(channel).wait_send()
        final_copy(channel).wait_send()
        sent = tiles.at[channel, pl.ds(0, 2 * CHIPS - 2)]
        copy_here(sent, sent, go_send.at[channel]).wait()
        copy_here(sent, sent, ret_send.at[channel]).wait()
        copy_here(out.at[channel], out_h.at[channel], out_sem.at[channel]).wait()


def local(model, dirty, psf, step_size, gain, w_in, b_in, w_out, kernel):
    rows_in, cols_in, cols_out, rows_out, swap, order = make_tables()
    smem = pl.BlockSpec(memory_space=pltpu.SMEM)
    vmem = pl.BlockSpec(memory_space=pltpu.VMEM)
    hbm = pl.BlockSpec(memory_space=pl.ANY)
    dma = pltpu.SemaphoreType.DMA
    steps = LEN // STEP_COLS
    return pl.pallas_call(
        whole,
        out_shape=jax.ShapeDtypeStruct((2, IMG, IMG), BF16),
        in_specs=[smem] * 2 + [hbm] * 7 + [vmem] * 6,
        out_specs=hbm,
        scratch_shapes=[
            pltpu.VMEM((2, IMG, IMG), BF16),
            pltpu.VMEM((2, IMG, IMG), BF16),
            pltpu.VMEM((2, PSF, PSF), BF16),
            pltpu.VMEM(rows_in.shape, BF16),
            pltpu.VMEM(cols_in.shape, BF16),
            pltpu.VMEM(cols_out.shape, BF16),
            pltpu.VMEM(rows_out.shape, BF16),
            pltpu.VMEM((HALF, 2 * IMG), BF16),
            pltpu.VMEM((HALF, 2 * PSF), BF16),
            pltpu.VMEM((steps, HALF, 2 * STEP_COLS), BF16),
            pltpu.VMEM((LEN, IMG), BF16),
            pltpu.VMEM((2, IMG, IMG), BF16),
            pltpu.VMEM((2, 2, IMG, 256), BF16),
            pltpu.VMEM((2, IMG, 256), BF16),
            pltpu.VMEM((2, 128, TILE, LANES), BF16),
            pltpu.VMEM((2, TILE // 2, 128, 256), BF16),
            pltpu.VMEM((TILE // 2, 256, 256), F32),
            pltpu.VMEM((TILE, LANES), F32),
            pltpu.VMEM((2, 128, TILE, LANES), BF16),
            pltpu.VMEM((2, 2, IMG, 256), BF16),
            pltpu.VMEM((2, IMG, IMG), BF16),
            pltpu.VMEM((2, IMG, IMG), BF16),
            pltpu.VMEM((IMG + 16, IMG), F32),
            dma((8,)),
        ]
        + [dma((2,))] * 9,
        compiler_params=pltpu.CompilerParams(
            vmem_limit_bytes=64 << 20, collective_id=0, has_side_effects=True
        ),
    )(
        step_size, kernel, model, dirty, psf, rows_in, cols_in, cols_out, rows_out,
        swap, order, gain[None, :], w_in, b_in[None, :], w_out,
    )


def solution(mesh):
    split = P(("rows", "cols"), None, None)
    return jax.shard_map(
        local,
        mesh=mesh,
        in_specs=(split, split, split, P(("rows", "cols")), P(), P(), P(), P(), P()),
        out_specs=split,
        check_vma=False,
    )
```

```python
import math

import jax
import jax.numpy as jnp
import ml_dtypes
import numpy as np
from jax import lax
from jax.experimental import pallas as pl
from jax.experimental.pallas import tpu as pltpu
from jax.sharding import PartitionSpec as P

BF16 = jnp.bfloat16
F32 = jnp.float32
MESH = pl.DeviceIdType.MESH
IMG = 512
PSF = 256
LEN = IMG + PSF // 2
HALF = LEN // 2
TILE = 16
LANES = 128
CHIPS = 64
STEP_COLS = 128


def angle(freq, place):
    turns = (2.0 * freq[:, None]) * place[None, :]
    return np.mod(turns, 2 * LEN) * (math.pi / LEN)


def make_tables():
    odd = np.arange(HALF) + 0.5
    even = np.arange(LEN).astype(np.float64)
    place = np.arange(IMG).astype(np.float64)
    window = place + PSF // 2
    first = angle(odd, place)
    rows_in = np.concatenate([np.cos(first), -np.sin(first)], axis=0)
    second = angle(even, place).T
    parts = []
    for start in range(0, LEN, STEP_COLS):
        cos = np.cos(second[:, start : start + STEP_COLS])
        sin = np.sin(second[:, start : start + STEP_COLS])
        parts.append(
            np.concatenate(
                [np.concatenate([cos, -sin], axis=1), np.concatenate([sin, cos], axis=1)], axis=0
            )
        )
    cols_in = np.stack(parts)
    back = angle(even, window)
    parts = []
    for start in range(0, LEN, STEP_COLS):
        cos = np.cos(back[start : start + STEP_COLS])
        sin = np.sin(back[start : start + STEP_COLS])
        parts.append(np.concatenate([cos, sin], axis=1))
        parts.append(np.concatenate([-sin, cos], axis=1))
    cols_out = np.concatenate(parts, axis=0)
    cols_out = np.stack(np.split(cols_out, 4, axis=1))
    last = angle(odd, window).T
    rows_out = np.concatenate([2 * np.cos(last), -2 * np.sin(last)], axis=1)
    swap = np.zeros((256, 256))
    index = np.arange(256)
    swap[index, (index % 16) * 16 + index // 16] = 1
    order = np.zeros((256, 256))
    order[index, (index % 2) * 128 + (index // 2 % 2) * CHIPS + index // 4] = 1
    tables = (rows_in, cols_in, cols_out, rows_out, swap, order)
    return [x.astype(ml_dtypes.bfloat16) for x in tables]


def dot(a, b):
    return jnp.dot(a, b, preferred_element_type=F32)


def copy_here(src, dst, sem):
    return pltpu.make_async_copy(src, dst, sem)


def first_axis(plane, psf, rows_in, image, point):
    low = dot(rows_in[...], plane[...]).astype(BF16)
    image[:, :IMG] = low[:HALF]
    image[:, IMG:] = low[HALF:]
    low = dot(rows_in[:, :PSF], psf[...]).astype(BF16)
    point[:, :PSF] = low[:HALF]
    point[:, PSF:] = low[HALF:]


def second_axis(cols_in, image, point, prod):
    def columns(step, carry):
        tab = cols_in.at[step]
        x = dot(image[...], tab[...])
        q = dot(point[:, :PSF], tab[:PSF]) + dot(point[:, PSF:], tab[IMG : IMG + PSF])
        x = x * (1.0 / (LEN * LEN))
        real_x, imag_x = x[:, :STEP_COLS], x[:, STEP_COLS:]
        real_q, imag_q = q[:, :STEP_COLS], q[:, STEP_COLS:]
        prod[step, :, :STEP_COLS] = (real_x * real_q - imag_x * imag_q).astype(BF16)
        prod[step, :, STEP_COLS:] = (real_x * imag_q + imag_x * real_q).astype(BF16)
        return carry

    lax.fori_loop(0, LEN // STEP_COLS, columns, 0, unroll=True)


def second_axis_back(cols_out, prod, back):
    for part in range(4):
        tab = cols_out.at[part]
        total = dot(prod[0], tab[: 2 * STEP_COLS])
        for step in range(1, LEN // STEP_COLS):
            total += dot(prod[step], tab[2 * STEP_COLS * step : 2 * STEP_COLS * (step + 1)])
        row, col = divmod(part, 2)
        back[row * HALF : (row + 1) * HALF, col * 256 : (col + 1) * 256] = total.astype(BF16)


def filter_plane(mixed, stepped, taps, out, wide):
    zero = jnp.zeros((8, IMG), F32)
    wide[:8] = zero
    wide[8 + IMG :] = zero

    def widen(step, carry):
        at = pl.multiple_of(step * 64, 64)
        wide[pl.ds(at + 8, 64), :] = mixed[pl.ds(at, 64), :].astype(F32)
        return carry

    lax.fori_loop(0, IMG // 64, widen, 0, unroll=4)
    rows = 32
    lane = lax.broadcasted_iota(jnp.int32, (rows, IMG), 1)

    def block(step, carry):
        at = pl.multiple_of(step * rows, rows)
        span = wide[pl.ds(at, rows + 16), :]
        lines = [span[7 + a : 7 + a + rows] for a in range(3)]
        sums = [sum(taps(a, b) * lines[a] for a in range(3)) for b in range(3)]
        left = jnp.where(lane == 0, 0.0, pltpu.roll(sums[0], 1, 1))
        right = jnp.where(lane == IMG - 1, 0.0, pltpu.roll(sums[2], IMG - 1, 1))
        total = stepped[pl.ds(at, rows), :].astype(F32) + (sums[1] + (left + right))
        out[pl.ds(at, rows), :] = total.astype(BF16)
        return carry

    lax.fori_loop(0, IMG // rows, block, 0, unroll=4)


def whole(
    rate_h, taps_h, model_h, dirty_h, psf_h, rows_in_h, cols_in_h, cols_out_h, rows_out_h,
    swap_h, order_h, gain_h, w_in_h, b_in_h, w_out_h, out_h,
    rate, taps, swap, order, gain, w_in, b_in, w_out,
    model, dirty, psf, rows_in, cols_in, cols_out, rows_out,
    image, point, prod, back, stepped, halves, parcel, tiles, turned, inner, scale,
    mixed, joined, planes, out, wide,
    load_sem, out_sem, pair_send, pair_recv, go_send, go_recv, ret_send, ret_recv, fin_send, fin_recv,
):
    row_at, col_at = lax.axis_index("rows"), lax.axis_index("cols")
    chip = row_at * 8 + col_at // 2
    core = col_at % 2
    sibling = {"rows": row_at, "cols": col_at + 1 - 2 * core}

    def at_chip(other):
        return {"rows": other // 8, "cols": (other % 8) * 2 + core}

    loads = []
    for src, dst in (
        (rows_in_h, rows_in),
        (model_h.at[0], model.at[0]),
        (psf_h, psf),
        (cols_in_h, cols_in),
        (cols_out_h, cols_out),
        (rows_out_h, rows_out),
        (dirty_h, dirty),
        (model_h.at[1], model.at[1]),
        (rate_h, rate),
        (swap_h, swap),
        (order_h, order),
        (gain_h, gain),
        (w_in_h, w_in),
        (b_in_h, b_in),
        (w_out_h, w_out),
        (taps_h, taps),
    ):
        copy = copy_here(src, dst, load_sem.at[len(loads)])
        copy.start()
        loads.append(copy)

    barrier = pltpu.get_barrier_semaphore()
    pl.semaphore_signal(barrier, inc=1, device_id=sibling, device_id_type=MESH)

    def greet(k, carry):
        pl.semaphore_signal(barrier, inc=1, device_id=at_chip(chip ^ k), device_id_type=MESH)
        return carry

    lax.fori_loop(1, CHIPS, greet, 0)

    def last_axis(channel):
        def rows(step, carry):
            at = pl.ds(pl.multiple_of(step * 128, 128), 128)
            blurred = dot(rows_out[at, :], back[...])
            held = model[channel, at, :].astype(F32)
            ahead = held + rate[channel] * (dirty[channel, at, :].astype(F32) - blurred)
            ahead = ahead.astype(BF16)
            stepped[channel, at, :] = ahead
            first = jnp.concatenate([ahead[:, :128], ahead[:, 256:384]], axis=1)
            second = jnp.concatenate([ahead[:, 128:256], ahead[:, 384:]], axis=1)
            halves[channel, core, at, :] = jnp.where(core == 0, first, second)
            parcel[channel, at, :] = jnp.where(core == 0, second, first)
            return carry

        lax.fori_loop(0, IMG // 128, rows, 0, unroll=True)

    def pair_copy(channel):
        return pltpu.make_async_remote_copy(
            src_ref=parcel.at[channel],
            dst_ref=halves.at[channel, core],
            send_sem=pair_send.at[channel],
            recv_sem=pair_recv.at[channel],
            device_id=sibling,
            device_id_type=MESH,
        )

    def tile_of(planes_ref, other):
        at = pl.ds(pl.multiple_of((other // 2) * TILE, TILE), TILE)
        return planes_ref.at[:, at, pl.ds(pl.multiple_of((other % 2) * LANES, LANES), LANES)]

    def place_of(plane_ref, other):
        at = pl.ds(pl.multiple_of((other // 2) * TILE, TILE), TILE)
        return plane_ref.at[at, pl.ds(pl.multiple_of((other % 2) * 256, 256), 256)]

    core_lanes = pl.ds(pl.multiple_of(core * LANES, LANES), LANES)

    def send_tiles(channel):
        def send(k, carry):
            other = chip ^ k
            pltpu.make_async_remote_copy(
                src_ref=tile_of(halves.at[channel], other),
                dst_ref=tiles.at[channel, :, chip],
                send_sem=go_send.at[channel],
                recv_sem=go_recv.at[channel],
                device_id=at_chip(other),
                device_id_type=MESH,
            ).start()
            return carry

        lax.fori_loop(1, CHIPS, send, 0)
        copy_here(
            tile_of(halves.at[channel], chip),
            tiles.at[channel, :, chip],
            go_recv.at[channel],
        ).start()

    def return_tiles(channel):
        def send(k, carry):
            other = chip ^ k
            pltpu.make_async_remote_copy(
                src_ref=joined.at[channel, other],
                dst_ref=place_of(planes.at[channel], chip),
                send_sem=ret_send.at[channel],
                recv_sem=ret_recv.at[channel],
                device_id=at_chip(other),
                device_id_type=MESH,
            ).start()
            return carry

        lax.fori_loop(1, CHIPS, send, 0)
        copy_here(
            joined.at[channel, chip],
            place_of(planes.at[channel], chip),
            ret_recv.at[channel],
        ).start()

    def swap_mixed(channel):
        return pltpu.make_async_remote_copy(
            src_ref=mixed.at[channel],
            dst_ref=joined.at[channel, :, :, core_lanes],
            send_sem=fin_send.at[channel],
            recv_sem=fin_recv.at[channel],
            device_id=sibling,
            device_id_type=MESH,
        )

    for load in loads[:3]:
        load.wait()
    first_axis(model.at[0], psf.at[0], rows_in, image, point)
    loads[3].wait()
    second_axis(cols_in, image, point, prod)
    loads[4].wait()
    second_axis_back(cols_out, prod, back)
    loads[5].wait()
    loads[6].wait()
    loads[8].wait()
    last_axis(0)
    pl.semaphore_wait(barrier, CHIPS)
    pair_copy(0).start()
    loads[7].wait()
    first_axis(model.at[1], psf.at[1], rows_in, image, point)
    pair_copy(0).wait_recv()
    send_tiles(0)
    second_axis(cols_in, image, point, prod)
    second_axis_back(cols_out, prod, back)
    last_axis(1)
    pair_copy(1).start()

    for load in loads[9:]:
        load.wait()
    w_in_t = (w_in[...].astype(F32).T * gain[...]).astype(BF16)
    w_in_t = dot(w_in_t, order[...]).astype(BF16)
    w_out_t = dot(w_out[...], order[...]).T.astype(BF16)
    bias = jnp.broadcast_to(b_in[...], (LANES, 256)).T
    bias = jnp.concatenate([bias, bias], axis=1)

    pair_copy(1).wait_recv()
    send_tiles(1)

    def power_of(channel, total):
        def add(group, total):
            v = tiles[channel, group // 4, pl.ds(pl.multiple_of((group % 4) * 16, 16), 16)].astype(F32)
            return total + jnp.sum(v * v, axis=0)

        return lax.fori_loop(0, 8, add, total, unroll=True)

    def turn(channel):
        def pairs(pair, carry):
            sides = [
                tiles[
                    channel, pair // 2, pl.ds(pl.multiple_of(pair % 2 * 32 + side * 16, 16), 16)
                ].reshape(256, LANES)
                for side in range(2)
            ]
            moved = dot(swap[...], jnp.concatenate(sides, axis=1)).astype(BF16)
            for side in range(2):
                at = pl.ds(pl.multiple_of(pair * 32 + side * 16, 16), 16)
                for r in range(TILE):
                    turned[channel, r // 2, at, (r % 2) * LANES : (r % 2 + 1) * LANES] = moved[
                        r * 16 : (r + 1) * 16, side * LANES : (side + 1) * LANES
                    ]
            return carry

        lax.fori_loop(0, 4, pairs, 0, unroll=True)

    def turn_back(channel, which, put):
        def pairs(pair, carry):
            sides = []
            for side in range(2):
                at = pl.ds(pl.multiple_of(which * CHIPS + pair * 32 + side * 16, 16), 16)
                lines = [
                    turned[channel, r // 2, at, (r % 2) * LANES : (r % 2 + 1) * LANES]
                    for r in range(TILE)
                ]
                sides.append(jnp.concatenate(lines, axis=0))
            moved = dot(swap[...], jnp.concatenate(sides, axis=1)).astype(BF16)
            for side in range(2):
                at = pl.ds(pl.multiple_of(pair * 32 + side * 16, 16), 16)
                put(at, moved[:, side * LANES : (side + 1) * LANES].reshape(16, TILE, LANES))
            return carry

        lax.fori_loop(0, 2, pairs, 0, unroll=True)

    def turn_back_other(channel):
        def put(at, block):
            mixed[channel, at] = block

        turn_back(channel, 1 - core, put)
        swap_mixed(channel).start()

    def turn_back_own(channel):
        def put(at, block):
            joined[channel, at, :, core_lanes] = block

        turn_back(channel, core, put)

    copy_here(tiles.at[0], tiles.at[0], go_recv.at[0]).wait()
    power = power_of(0, jnp.zeros((TILE, LANES), F32))
    turn(0)

    def layer_part(pair, carry):
        inner[pair] = dot(w_in_t[:, :128], turned[0, pair])
        return carry

    lax.fori_loop(0, TILE // 2, layer_part, 0, unroll=True)
    copy_here(tiles.at[1], tiles.at[1], go_recv.at[1]).wait()
    power = power_of(1, power)
    scale[...] = lax.rsqrt(power * (1.0 / 256) + 1e-06)
    turn(1)

    def layers(pair, carry):
        factor = jnp.concatenate([scale[pl.ds(2 * pair, 1), :], scale[pl.ds(2 * pair + 1, 1), :]], axis=1)
        total = inner[pair] + dot(w_in_t[:, 128:], turned[1, pair])
        hidden = jax.nn.gelu(total * factor + bias, approximate=True).astype(BF16)
        result = dot(w_out_t, hidden).astype(BF16)
        turned[0, pair] = result[:128]
        turned[1, pair] = result[128:]
        return carry

    lax.fori_loop(0, TILE // 2, layers, 0, unroll=True)
    turn_back_other(0)
    turn_back_other(1)
    turn_back_own(0)
    swap_mixed(0).wait_recv()
    return_tiles(0)
    turn_back_own(1)
    swap_mixed(1).wait_recv()
    return_tiles(1)

    for channel in range(2):
        copy_here(planes.at[channel], planes.at[channel], ret_recv.at[channel]).wait()
        filter_plane(
            planes.at[channel], stepped.at[channel],
            lambda a, b: taps[a, b, (chip * 2 + core) * 2 + channel], out.at[channel], wide,
        )
        copy_here(out.at[channel], out_h.at[channel], out_sem.at[channel]).start()
    for channel in range(2):
        pair_copy(channel).wait_send()
        swap_mixed(channel).wait_send()
        sent = tiles.at[channel, :, pl.ds(0, CHIPS - 1)]
        copy_here(sent, sent, go_send.at[channel]).wait()
        copy_here(sent, sent, ret_send.at[channel]).wait()
        copy_here(out.at[channel], out_h.at[channel], out_sem.at[channel]).wait()


def local(model, dirty, psf, step_size, gain, w_in, b_in, w_out, kernel):
    rows_in, cols_in, cols_out, rows_out, swap, order = make_tables()
    hbm = pl.BlockSpec(memory_space=pl.ANY)
    dma = pltpu.SemaphoreType.DMA
    steps = LEN // STEP_COLS
    return pl.pallas_call(
        whole,
        out_shape=jax.ShapeDtypeStruct((2, IMG, IMG), BF16),
        in_specs=[hbm] * 15,
        out_specs=hbm,
        scratch_shapes=[
            pltpu.SMEM((2,), F32),
            pltpu.SMEM((3, 3, 256), F32),
            pltpu.VMEM((256, 256), BF16),
            pltpu.VMEM((256, 256), BF16),
            pltpu.VMEM((1, 256), F32),
            pltpu.VMEM((256, 256), BF16),
            pltpu.VMEM((1, 256), F32),
            pltpu.VMEM((256, 256), BF16),
            pltpu.VMEM((2, IMG, IMG), BF16),
            pltpu.VMEM((2, IMG, IMG), BF16),
            pltpu.VMEM((2, PSF, PSF), BF16),
            pltpu.VMEM(rows_in.shape, BF16),
            pltpu.VMEM(cols_in.shape, BF16),
            pltpu.VMEM(cols_out.shape, BF16),
            pltpu.VMEM(rows_out.shape, BF16),
            pltpu.VMEM((HALF, 2 * IMG), BF16),
            pltpu.VMEM((HALF, 2 * PSF), BF16),
            pltpu.VMEM((steps, HALF, 2 * STEP_COLS), BF16),
            pltpu.VMEM((LEN, IMG), BF16),
            pltpu.VMEM((2, IMG, IMG), BF16),
            pltpu.VMEM((2, 2, IMG, 256), BF16),
            pltpu.VMEM((2, IMG, 256), BF16),
            pltpu.VMEM((2, 2, CHIPS, TILE, LANES), BF16),
            pltpu.VMEM((2, TILE // 2, 128, 256), BF16),
            pltpu.VMEM((TILE // 2, 256, 256), F32),
            pltpu.VMEM((TILE, LANES), F32),
            pltpu.VMEM((2, CHIPS, TILE, LANES), BF16),
            pltpu.VMEM((2, CHIPS, TILE, 2 * LANES), BF16),
            pltpu.VMEM((2, IMG, IMG), BF16),
            pltpu.VMEM((2, IMG, IMG), BF16),
            pltpu.VMEM((IMG + 16, IMG), F32),
            dma((16,)),
        ]
        + [dma((2,))] * 9,
        compiler_params=pltpu.CompilerParams(
            vmem_limit_bytes=64 << 20, collective_id=0, has_side_effects=True
        ),
    )(
        step_size, kernel, model, dirty, psf, rows_in, cols_in, cols_out, rows_out,
        swap, order, gain[None, :], w_in, b_in[None, :], w_out,
    )


def solution(mesh):
    split = P(("rows", "cols"), None, None)
    return jax.shard_map(
        local,
        mesh=mesh,
        in_specs=(split, split, split, P(("rows", "cols")), P(), P(), P(), P(), P()),
        out_specs=split,
        check_vma=False,
    )
```

```python
import math

import jax
import jax.numpy as jnp
import ml_dtypes
import numpy as np
from jax import lax
from jax.experimental import pallas as pl
from jax.experimental.pallas import tpu as pltpu
from jax.sharding import PartitionSpec as P

BF16 = jnp.bfloat16
F32 = jnp.float32
MESH = pl.DeviceIdType.MESH
IMG = 512
PSF = 256
LEN = IMG + PSF // 2
HALF = LEN // 2
TILE = 16
LANES = 128
CHIPS = 64
FIVE = LEN // LANES


def angle(freq, place):
    turns = (2.0 * freq[:, None]) * place[None, :]
    return np.mod(turns, 2 * LEN) * (math.pi / LEN)


def make_tables():
    odd = np.arange(HALF) + 0.5
    even = np.arange(LEN).astype(np.float64)
    place = np.arange(IMG).astype(np.float64)
    window = place + PSF // 2
    first = angle(odd, place)
    rows_in = np.concatenate([np.cos(first), -np.sin(first)], axis=0)
    inside = np.arange(LANES).astype(np.float64)
    cols_in, cols_out = [], []
    for shift in range(FIVE):
        second = angle(even[shift::FIVE], inside)
        cos, sin = np.cos(second.T), np.sin(second.T)
        cols_in.append(np.block([[cos, -sin], [sin, cos]]))
        cos, sin = np.cos(second), np.sin(second)
        cols_out.append(np.block([[cos, sin], [-sin, cos]]))
    cols_in, cols_out = np.stack(cols_in), np.stack(cols_out)
    last = angle(odd, window).T
    rows_out = np.concatenate([2 * np.cos(last), -2 * np.sin(last)], axis=1)
    swap = np.zeros((256, 256))
    index = np.arange(256)
    swap[index, (index % 16) * 16 + index // 16] = 1
    order = np.zeros((256, 256))
    order[index, (index % 2) * 128 + (index // 2 % 2) * CHIPS + index // 4] = 1
    tables = (rows_in, cols_in, cols_out, rows_out, swap, order)
    return [x.astype(ml_dtypes.bfloat16) for x in tables]


def dot(a, b):
    return jnp.dot(a, b, preferred_element_type=F32)


def copy_here(src, dst, sem):
    return pltpu.make_async_copy(src, dst, sem)


COS = [math.cos(2 * math.pi * k / FIVE) for k in range(FIVE)]
SIN = [math.sin(2 * math.pi * k / FIVE) for k in range(FIVE)]


def combine(zero, ones, real_even, imag_odd):
    even = [zero[p] + ones[0] * real_even[0][p] + ones[1] * real_even[1][p] for p in range(2)]
    odd = [ones[2] * imag_odd[0][p] + ones[3] * imag_odd[1][p] for p in range(2)]
    plus = (even[0] - odd[1], even[1] + odd[0])
    minus = (even[0] + odd[1], even[1] - odd[0])
    return plus, minus


def spread_five(x):
    both = [x[2][p] + x[3][p] for p in range(2)]
    apart = [x[2][p] - x[3][p] for p in range(2)]
    fourth, first = combine(x[0], (COS[1], COS[2], SIN[1], SIN[2]), (x[1], both), (x[1], apart))
    third, second = combine(x[0], (COS[2], COS[1], SIN[2], -SIN[1]), (x[1], both), (x[1], apart))
    zeroth = tuple(x[0][p] + x[1][p] + both[p] for p in range(2))
    return zeroth, first, second, third, fourth


def spread_two(x):
    out = [tuple(x[0][p] + x[1][p] for p in range(2))]
    for r in range(1, FIVE):
        out.append(
            (
                x[0][0] + COS[r] * x[1][0] + SIN[r] * x[1][1],
                x[0][1] + COS[r] * x[1][1] - SIN[r] * x[1][0],
            )
        )
    return out


def gather_five(z):
    sums = [[z[k][p] + z[FIVE - k][p] for p in range(2)] for k in (1, 2)]
    gaps = [[z[k][p] - z[FIVE - k][p] for p in range(2)] for k in (1, 2)]
    first, fourth = combine(z[0], (COS[1], COS[2], SIN[1], SIN[2]), sums, gaps)
    second, third = combine(z[0], (COS[2], COS[1], SIN[2], -SIN[1]), sums, gaps)
    return first, second, third, fourth


def lane_blocks(ref, at_re, at_im, count):
    return [
        (ref[at_re, a * LANES : (a + 1) * LANES], ref[at_im, a * LANES : (a + 1) * LANES])
        for a in range(count)
    ]


def first_axis(plane, psf, rows_in, image, point, low, low_psf):
    low_psf[...] = dot(rows_in[:, :PSF], psf[...])
    low[...] = dot(rows_in[...], plane[...])

    def rows(step, carry):
        at = pl.multiple_of(step * 16, 16)
        at_re, at_im = pl.ds(at, 16), pl.ds(HALF + at, 16)
        for ref, out, spread in ((low_psf, point, spread_two), (low, image, spread_five)):
            parts = spread(lane_blocks(ref, at_re, at_im, ref.shape[1] // LANES))
            for r in range(FIVE):
                out[r, at_re, :LANES] = parts[r][0].astype(BF16)
                out[r, at_re, LANES:] = parts[r][1].astype(BF16)
        return carry

    lax.fori_loop(0, HALF // 16, rows, 0, unroll=4)


def second_axis(cols_in, cols_out, image, point, spectra):
    for r in range(FIVE):
        x = dot(image[r], cols_in[r]) * (1.0 / (LEN * LEN))
        q = dot(point[r], cols_in[r])
        real_x, imag_x = x[:, :LANES], x[:, LANES:]
        real_q, imag_q = q[:, :LANES], q[:, LANES:]
        real_p = (real_x * real_q - imag_x * imag_q).astype(BF16)
        imag_p = (real_x * imag_q + imag_x * real_q).astype(BF16)
        spectra[r] = dot(jnp.concatenate([real_p, imag_p], axis=1), cols_out[r])


def second_axis_back(spectra, back):
    def rows(step, carry):
        at = pl.multiple_of(step * 16, 16)
        here = pl.ds(at, 16)
        z = [(spectra[r, here, :LANES], spectra[r, here, LANES:]) for r in range(FIVE)]
        for a, (re, im) in enumerate(gather_five(z)):
            back[here, a * LANES : (a + 1) * LANES] = re.astype(BF16)
            back[pl.ds(HALF + at, 16), a * LANES : (a + 1) * LANES] = im.astype(BF16)
        return carry

    lax.fori_loop(0, HALF // 16, rows, 0, unroll=4)


def widen(units, half, wide):
    def some(step, carry):
        at = pl.multiple_of(step * 64, 64)
        v = units[pl.ds(at, 64), :].astype(F32).reshape(4, 2, 8, IMG)
        for channel in range(2):
            for g in range(4):
                wide[channel, pl.ds(at + g * 16 + half * 8 + 8, 8), :] = v[g, channel]
        return carry

    lax.fori_loop(0, IMG // 64, some, 0, unroll=4)


def filter_plane(stepped, taps, out, wide):
    rows = 32
    lane = lax.broadcasted_iota(jnp.int32, (rows, IMG), 1)

    def block(step, carry):
        at = pl.multiple_of(step * rows, rows)
        span = wide[pl.ds(at, rows + 16), :]
        lines = [span[7 + a : 7 + a + rows] for a in range(3)]
        sums = [sum(taps(a, b) * lines[a] for a in range(3)) for b in range(3)]
        left = jnp.where(lane == 0, 0.0, pltpu.roll(sums[0], 1, 1))
        right = jnp.where(lane == IMG - 1, 0.0, pltpu.roll(sums[2], IMG - 1, 1))
        total = stepped[pl.ds(at, rows), :].astype(F32) + (sums[1] + (left + right))
        out[pl.ds(at, rows), :] = total.astype(BF16)
        return carry

    lax.fori_loop(0, IMG // rows, block, 0, unroll=4)


def whole(
    rate_h, taps_h, model_h, dirty_h, psf_h, rows_in_h, cols_in_h, cols_out_h, rows_out_h,
    swap_h, order_h, gain_h, w_in_h, b_in_h, w_out_h, out_h,
    rate, taps, swap, order, gain, w_in, b_in, w_out,
    model, dirty, psf, rows_in, cols_in, cols_out, rows_out,
    low, low_psf, image, point, spectra, back, stepped, halves, parcel, tiles, turned,
    mixed, joined, planes, out, wide,
    load_sem, out_sem, pair_send, pair_recv, go_send, go_recv, ret_send, ret_recv, fin_send, fin_recv,
):
    row_at, col_at = lax.axis_index("rows"), lax.axis_index("cols")
    chip = row_at * 8 + col_at // 2
    core = col_at % 2
    sibling = {"rows": row_at, "cols": col_at + 1 - 2 * core}

    def at_chip(other):
        return {"rows": other // 8, "cols": (other % 8) * 2 + core}

    loads = []
    for src, dst in (
        (rows_in_h, rows_in),
        (model_h.at[0], model.at[0]),
        (psf_h, psf),
        (cols_in_h, cols_in),
        (cols_out_h, cols_out),
        (rows_out_h, rows_out),
        (dirty_h, dirty),
        (model_h.at[1], model.at[1]),
        (rate_h, rate),
        (swap_h, swap),
        (order_h, order),
        (gain_h, gain),
        (w_in_h, w_in),
        (b_in_h, b_in),
        (w_out_h, w_out),
        (taps_h, taps),
    ):
        copy = copy_here(src, dst, load_sem.at[len(loads)])
        copy.start()
        loads.append(copy)

    barrier = pltpu.get_barrier_semaphore()
    pl.semaphore_signal(barrier, inc=1, device_id=sibling, device_id_type=MESH)

    def greet(k, carry):
        pl.semaphore_signal(barrier, inc=1, device_id=at_chip(chip ^ k), device_id_type=MESH)
        return carry

    lax.fori_loop(1, CHIPS, greet, 0)

    def pair_copy(half, at):
        return pltpu.make_async_remote_copy(
            src_ref=parcel.at[half, at],
            dst_ref=halves.at[half, core, at],
            send_sem=pair_send.at[half],
            recv_sem=pair_recv.at[half],
            device_id=sibling,
            device_id_type=MESH,
        )

    def ahead(channel, at):
        blurred = dot(rows_out[at, :], back[...])
        held = model[channel, at, :].astype(F32)
        result = held + rate[channel] * (dirty[channel, at, :].astype(F32) - blurred)
        result = result.astype(BF16)
        stepped[channel, at, :] = result
        return result

    def pack(at):
        planes_at = [stepped[0, at, :].astype(F32), ahead(1, at).astype(F32)]
        planes_at = [v.reshape(8, 2, 8, IMG) for v in planes_at]
        for half in range(2):
            unit = jnp.stack([v[:, half] for v in planes_at], axis=1).reshape(128, IMG).astype(BF16)
            first = jnp.concatenate([unit[:, :128], unit[:, 256:384]], axis=1)
            second = jnp.concatenate([unit[:, 128:256], unit[:, 384:]], axis=1)
            halves[half, core, at, :] = jnp.where(core == 0, first, second)
            parcel[half, at, :] = jnp.where(core == 0, second, first)
        for half in range(2):
            pair_copy(half, at).start()

    def tile_of(planes_ref, other):
        at = pl.ds(pl.multiple_of((other // 2) * TILE, TILE), TILE)
        return planes_ref.at[:, at, pl.ds(pl.multiple_of((other % 2) * LANES, LANES), LANES)]

    def place_of(plane_ref, other):
        at = pl.ds(pl.multiple_of((other // 2) * TILE, TILE), TILE)
        return plane_ref.at[at, pl.ds(pl.multiple_of((other % 2) * 256, 256), 256)]

    core_lanes = pl.ds(pl.multiple_of(core * LANES, LANES), LANES)

    def send_tiles(channel):
        def send(k, carry):
            other = chip ^ k
            pltpu.make_async_remote_copy(
                src_ref=tile_of(halves.at[channel], other),
                dst_ref=tiles.at[channel, :, chip],
                send_sem=go_send.at[channel],
                recv_sem=go_recv.at[channel],
                device_id=at_chip(other),
                device_id_type=MESH,
            ).start()
            return carry

        lax.fori_loop(1, CHIPS, send, 0)
        copy_here(
            tile_of(halves.at[channel], chip),
            tiles.at[channel, :, chip],
            go_recv.at[channel],
        ).start()

    def return_tiles(channel):
        def send(k, carry):
            other = chip ^ k
            pltpu.make_async_remote_copy(
                src_ref=joined.at[channel, other],
                dst_ref=place_of(planes.at[channel], chip),
                send_sem=ret_send.at[channel],
                recv_sem=ret_recv.at[channel],
                device_id=at_chip(other),
                device_id_type=MESH,
            ).start()
            return carry

        lax.fori_loop(1, CHIPS, send, 0)
        copy_here(
            joined.at[channel, chip],
            place_of(planes.at[channel], chip),
            ret_recv.at[channel],
        ).start()

    def swap_mixed(channel):
        return pltpu.make_async_remote_copy(
            src_ref=mixed.at[channel],
            dst_ref=joined.at[channel, :, :, core_lanes],
            send_sem=fin_send.at[channel],
            recv_sem=fin_recv.at[channel],
            device_id=sibling,
            device_id_type=MESH,
        )

    for load in loads[:3]:
        load.wait()
    first_axis(model.at[0], psf.at[0], rows_in, image, point, low, low_psf)
    loads[3].wait()
    loads[4].wait()
    second_axis(cols_in, cols_out, image, point, spectra)
    second_axis_back(spectra, back)
    loads[5].wait()
    loads[6].wait()
    loads[8].wait()
    blocks = [pl.ds(step * 128, 128) for step in range(IMG // 128)]
    for at in blocks:
        ahead(0, at)
    loads[7].wait()
    first_axis(model.at[1], psf.at[1], rows_in, image, point, low, low_psf)
    second_axis(cols_in, cols_out, image, point, spectra)
    second_axis_back(spectra, back)
    pl.semaphore_wait(barrier, CHIPS)
    for at in blocks:
        pack(at)
    for half in range(2):
        copy_here(parcel.at[half], parcel.at[half], pair_recv.at[half]).wait()
        send_tiles(half)

    for load in loads[9:]:
        load.wait()
    w_in_t = (w_in[...].astype(F32).T * gain[...]).astype(BF16)
    w_in_t = dot(w_in_t, order[...]).astype(BF16)
    w_out_t = dot(w_out[...], order[...]).T.astype(BF16)
    bias = jnp.broadcast_to(b_in[...], (LANES, 256)).T
    bias = jnp.concatenate([bias, bias], axis=1)

    def scale_of(half):
        total = jnp.zeros((TILE, LANES), F32)
        for group in range(8):
            v = tiles[half, group // 4, pl.ds(group % 4 * 16, 16)].astype(F32)
            total = total + jnp.sum(v * v, axis=0)
        return lax.rsqrt((total[:8] + total[8:]) * (1.0 / 256) + 1e-06)

    def turn(half):
        for pair in range(4):
            sides = [
                tiles[half, pair // 2, pl.ds(pair % 2 * 32 + side * 16, 16)].reshape(256, LANES)
                for side in range(2)
            ]
            moved = dot(swap[...], jnp.concatenate(sides, axis=1)).astype(BF16)
            for side in range(2):
                for line in range(TILE):
                    channel, r = divmod(line, 8)
                    at = pl.ds(channel * 128 + pair * 32 + side * 16, 16)
                    turned[half, r // 2, at, (r % 2) * LANES : (r % 2 + 1) * LANES] = moved[
                        line * 16 : (line + 1) * 16, side * LANES : (side + 1) * LANES
                    ]

    def layers(half):
        scale = scale_of(half)
        for pair in range(4):
            factor = jnp.concatenate(
                [scale[2 * pair : 2 * pair + 1], scale[2 * pair + 1 : 2 * pair + 2]], axis=1
            )
            total = dot(w_in_t, turned[half, pair])
            hidden = jax.nn.gelu(total * factor + bias, approximate=True).astype(BF16)
            turned[half, pair] = dot(w_out_t, hidden).astype(BF16)

    def turn_back(half, which, put):
        for pair in range(2):
            sides = []
            for side in range(2):
                lines = []
                for line in range(TILE):
                    channel, r = divmod(line, 8)
                    first = channel * 128 + pair * 32 + side * 16
                    at = pl.ds(pl.multiple_of(which * CHIPS + first, 16), 16)
                    lines.append(turned[half, r // 2, at, (r % 2) * LANES : (r % 2 + 1) * LANES])
                sides.append(jnp.concatenate(lines, axis=0))
            moved = dot(swap[...], jnp.concatenate(sides, axis=1)).astype(BF16)
            for side in range(2):
                block = moved[:, side * LANES : (side + 1) * LANES].reshape(16, TILE, LANES)
                put(pl.ds(pair * 32 + side * 16, 16), block)

    def turn_back_other(half):
        def put(at, block):
            mixed[half, at] = block

        turn_back(half, 1 - core, put)
        swap_mixed(half).start()

    def turn_back_own(half):
        def put(at, block):
            joined[half, at, :, core_lanes] = block

        turn_back(half, core, put)

    for half in range(2):
        copy_here(tiles.at[half], tiles.at[half], go_recv.at[half]).wait()
        turn(half)
        layers(half)
        turn_back_other(half)
        turn_back_own(half)
        swap_mixed(half).wait_recv()
        return_tiles(half)

    zero = jnp.zeros((8, IMG), F32)
    for channel in range(2):
        wide[channel, :8] = zero
        wide[channel, 8 + IMG :] = zero
    for half in range(2):
        copy_here(planes.at[half], planes.at[half], ret_recv.at[half]).wait()
        widen(planes.at[half], half, wide)
    for channel in range(2):
        filter_plane(
            stepped.at[channel],
            lambda a, b: taps[a, b, (chip * 2 + core) * 2 + channel], out.at[channel], wide.at[channel],
        )
        copy_here(out.at[channel], out_h.at[channel], out_sem.at[channel]).start()
    for channel in range(2):
        copy_here(parcel.at[channel], parcel.at[channel], pair_send.at[channel]).wait()
        swap_mixed(channel).wait_send()
        sent = tiles.at[channel, :, pl.ds(0, CHIPS - 1)]
        copy_here(sent, sent, go_send.at[channel]).wait()
        copy_here(sent, sent, ret_send.at[channel]).wait()
        copy_here(out.at[channel], out_h.at[channel], out_sem.at[channel]).wait()


def local(model, dirty, psf, step_size, gain, w_in, b_in, w_out, kernel):
    rows_in, cols_in, cols_out, rows_out, swap, order = make_tables()
    hbm = pl.BlockSpec(memory_space=pl.ANY)
    dma = pltpu.SemaphoreType.DMA
    return pl.pallas_call(
        whole,
        out_shape=jax.ShapeDtypeStruct((2, IMG, IMG), BF16),
        in_specs=[hbm] * 15,
        out_specs=hbm,
        scratch_shapes=[
            pltpu.SMEM((2,), F32),
            pltpu.SMEM((3, 3, 256), F32),
            pltpu.VMEM((256, 256), BF16),
            pltpu.VMEM((256, 256), BF16),
            pltpu.VMEM((1, 256), F32),
            pltpu.VMEM((256, 256), BF16),
            pltpu.VMEM((1, 256), F32),
            pltpu.VMEM((256, 256), BF16),
            pltpu.VMEM((2, IMG, IMG), BF16),
            pltpu.VMEM((2, IMG, IMG), BF16),
            pltpu.VMEM((2, PSF, PSF), BF16),
            pltpu.VMEM(rows_in.shape, BF16),
            pltpu.VMEM(cols_in.shape, BF16),
            pltpu.VMEM(cols_out.shape, BF16),
            pltpu.VMEM(rows_out.shape, BF16),
            pltpu.VMEM((LEN, IMG), F32),
            pltpu.VMEM((LEN, PSF), F32),
            pltpu.VMEM((FIVE, HALF, 2 * LANES), BF16),
            pltpu.VMEM((FIVE, HALF, 2 * LANES), BF16),
            pltpu.VMEM((FIVE, HALF, 2 * LANES), F32),
            pltpu.VMEM((LEN, IMG), BF16),
            pltpu.VMEM((2, IMG, IMG), BF16),
            pltpu.VMEM((2, 2, IMG, 256), BF16),
            pltpu.VMEM((2, IMG, 256), BF16),
            pltpu.VMEM((2, 2, CHIPS, TILE, LANES), BF16),
            pltpu.VMEM((2, TILE // 4, 256, 256), BF16),
            pltpu.VMEM((2, CHIPS, TILE, LANES), BF16),
            pltpu.VMEM((2, CHIPS, TILE, 2 * LANES), BF16),
            pltpu.VMEM((2, IMG, IMG), BF16),
            pltpu.VMEM((2, IMG, IMG), BF16),
            pltpu.VMEM((2, IMG + 16, IMG), F32),
            dma((16,)),
        ]
        + [dma((2,))] * 9,
        compiler_params=pltpu.CompilerParams(
            vmem_limit_bytes=64 << 20, collective_id=0, has_side_effects=True
        ),
    )(
        step_size, kernel, model, dirty, psf, rows_in, cols_in, cols_out, rows_out,
        swap, order, gain[None, :], w_in, b_in[None, :], w_out,
    )


def solution(mesh):
    split = P(("rows", "cols"), None, None)
    return jax.shard_map(
        local,
        mesh=mesh,
        in_specs=(split, split, split, P(("rows", "cols")), P(), P(), P(), P(), P()),
        out_specs=split,
        check_vma=False,
    )
```

```python
import math

import jax
import jax.numpy as jnp
import ml_dtypes
import numpy as np
from jax import lax
from jax.experimental import pallas as pl
from jax.experimental.pallas import tpu as pltpu
from jax.sharding import PartitionSpec as P

BF16 = jnp.bfloat16
F32 = jnp.float32
MESH = pl.DeviceIdType.MESH
IMG = 512
PSF = 256
LEN = IMG + PSF // 2
HALF = LEN // 2
PARTS = 4
BLOCKS = 4
TILE = 16
LANES = 128
CHIPS = 64
FIVE = LEN // LANES


def angle(freq, place):
    turns = (2.0 * freq[:, None]) * place[None, :]
    return np.mod(turns, 2 * LEN) * (math.pi / LEN)


def make_tables():
    odd = np.arange(HALF) + 0.5
    even = np.arange(LEN).astype(np.float64)
    place = np.arange(IMG).astype(np.float64)
    window = place + PSF // 2
    first = angle(odd, place)
    rows_in = np.concatenate([np.cos(first), -np.sin(first)], axis=0)
    inside = np.arange(LANES).astype(np.float64)
    cols_in, cols_out = [], []
    for shift in range(FIVE):
        second = angle(even[shift::FIVE], inside)
        cos, sin = np.cos(second.T), np.sin(second.T)
        cols_in.append(np.block([[cos, -sin], [sin, cos]]))
        cos, sin = np.cos(second), np.sin(second)
        cols_out.append(np.block([[cos, sin], [-sin, cos]]))
    cols_in, cols_out = np.stack(cols_in), np.stack(cols_out)
    last = angle(odd, window).T
    rows_out = np.concatenate([2 * np.cos(last), -2 * np.sin(last)], axis=1)
    swap = np.zeros((256, 256))
    index = np.arange(256)
    swap[index, (index % 16) * 16 + index // 16] = 1
    order = np.zeros((256, 256))
    order[index, (index % 2) * 128 + (index // 2 % 2) * CHIPS + index // 4] = 1
    tables = (rows_in, cols_in, cols_out, rows_out, swap, order)
    return [x.astype(ml_dtypes.bfloat16) for x in tables]


def dot(a, b):
    return jnp.dot(a, b, preferred_element_type=F32)


def copy_here(src, dst, sem):
    return pltpu.make_async_copy(src, dst, sem)


COS = [math.cos(2 * math.pi * k / FIVE) for k in range(FIVE)]
SIN = [math.sin(2 * math.pi * k / FIVE) for k in range(FIVE)]


def combine(zero, ones, real_even, imag_odd):
    even = [zero[p] + ones[0] * real_even[0][p] + ones[1] * real_even[1][p] for p in range(2)]
    odd = [ones[2] * imag_odd[0][p] + ones[3] * imag_odd[1][p] for p in range(2)]
    plus = (even[0] - odd[1], even[1] + odd[0])
    minus = (even[0] + odd[1], even[1] - odd[0])
    return plus, minus


def spread_five(x):
    both = [x[2][p] + x[3][p] for p in range(2)]
    apart = [x[2][p] - x[3][p] for p in range(2)]
    fourth, first = combine(x[0], (COS[1], COS[2], SIN[1], SIN[2]), (x[1], both), (x[1], apart))
    third, second = combine(x[0], (COS[2], COS[1], SIN[2], -SIN[1]), (x[1], both), (x[1], apart))
    zeroth = tuple(x[0][p] + x[1][p] + both[p] for p in range(2))
    return zeroth, first, second, third, fourth


def spread_two(x):
    out = [tuple(x[0][p] + x[1][p] for p in range(2))]
    for r in range(1, FIVE):
        out.append(
            (
                x[0][0] + COS[r] * x[1][0] + SIN[r] * x[1][1],
                x[0][1] + COS[r] * x[1][1] - SIN[r] * x[1][0],
            )
        )
    return out


def gather_five(z):
    sums = [[z[k][p] + z[FIVE - k][p] for p in range(2)] for k in (1, 2)]
    gaps = [[z[k][p] - z[FIVE - k][p] for p in range(2)] for k in (1, 2)]
    first, fourth = combine(z[0], (COS[1], COS[2], SIN[1], SIN[2]), sums, gaps)
    second, third = combine(z[0], (COS[2], COS[1], SIN[2], -SIN[1]), sums, gaps)
    return first, second, third, fourth


def lane_blocks(ref, at_re, at_im, count):
    return [
        (ref[at_re, a * LANES : (a + 1) * LANES], ref[at_im, a * LANES : (a + 1) * LANES])
        for a in range(count)
    ]


def first_axis(plane, psf, rows_in, image, point, low, low_psf):
    low_psf[...] = dot(rows_in[:, :PSF], psf[...])
    low[...] = dot(rows_in[...], plane[...])

    def rows(step, carry):
        at = pl.multiple_of(step * 16, 16)
        at_re, at_im = pl.ds(at, 16), pl.ds(HALF + at, 16)
        for ref, out, spread in ((low_psf, point, spread_two), (low, image, spread_five)):
            parts = spread(lane_blocks(ref, at_re, at_im, ref.shape[1] // LANES))
            for r in range(FIVE):
                out[r, at_re, :LANES] = parts[r][0].astype(BF16)
                out[r, at_re, LANES:] = parts[r][1].astype(BF16)
        return carry

    lax.fori_loop(0, HALF // 16, rows, 0, unroll=True)


def second_axis(cols_in, cols_out, image, point, spectra):
    for r in range(FIVE):
        x = dot(image[r], cols_in[r]) * (1.0 / (LEN * LEN))
        q = dot(point[r], cols_in[r])
        real_x, imag_x = x[:, :LANES], x[:, LANES:]
        real_q, imag_q = q[:, :LANES], q[:, LANES:]
        real_p = (real_x * real_q - imag_x * imag_q).astype(BF16)
        imag_p = (real_x * imag_q + imag_x * real_q).astype(BF16)
        spectra[r] = dot(jnp.concatenate([real_p, imag_p], axis=1), cols_out[r])


def second_axis_back(spectra, back):
    def rows(step, carry):
        at = pl.multiple_of(step * 16, 16)
        here = pl.ds(at, 16)
        z = [(spectra[r, here, :LANES], spectra[r, here, LANES:]) for r in range(FIVE)]
        for a, (re, im) in enumerate(gather_five(z)):
            back[here, a * LANES : (a + 1) * LANES] = re.astype(BF16)
            back[pl.ds(HALF + at, 16), a * LANES : (a + 1) * LANES] = im.astype(BF16)
        return carry

    lax.fori_loop(0, HALF // 16, rows, 0, unroll=True)


def filter_columns(units, half, taps, wide):
    lane = lax.broadcasted_iota(jnp.int32, (8, LANES), 1)
    zero = jnp.zeros((8, LANES), F32)
    weights = [[[taps(a, b, channel) for b in range(3)] for a in range(3)] for channel in range(2)]

    def some(step, carry):
        at = pl.multiple_of(step * 64, 64)
        v = units[pl.ds(at, 64), :].astype(F32).reshape(4, 2, 8, IMG)
        for channel in range(2):
            w = weights[channel]
            for g in range(4):
                to = pl.ds(at + g * 16 + half * 8 + 8, 8)
                m = [v[g, channel, :, j * LANES : (j + 1) * LANES] for j in range(BLOCKS)]
                left = [zero] + [pltpu.roll(x, 1, 1) for x in m]
                right = [pltpu.roll(x, LANES - 1, 1) for x in m] + [zero]
                for j in range(BLOCKS):
                    before = jnp.where(lane == 0, left[j], left[j + 1])
                    after = jnp.where(lane == LANES - 1, right[j + 1], right[j])
                    for a in range(3):
                        wide[a, channel, j, to, :] = (
                            w[a][0] * before + w[a][1] * m[j] + w[a][2] * after
                        )
        return carry

    lax.fori_loop(0, IMG // 64, some, 0, unroll=2)


def filter_rows(stepped, channel, out, wide, start, count):
    rows = 16

    def block(step, carry):
        at = pl.multiple_of(start + step * rows, rows)
        for j in range(BLOCKS):
            lines = [wide[a, channel, j, pl.ds(at + 7 + a, rows), :] for a in range(3)]
            lanes = slice(j * LANES, (j + 1) * LANES)
            total = stepped[pl.ds(at, rows), lanes].astype(F32) + (lines[0] + lines[1] + lines[2])
            out[pl.ds(at, rows), lanes] = total.astype(BF16)
        return carry

    lax.fori_loop(0, count // rows, block, 0, unroll=True)


def whole(
    rate_h, taps_h, model_h, dirty_h, psf_h, rows_in_h, cols_in_h, cols_out_h, rows_out_h,
    swap_h, order_h, gain_h, w_in_h, b_in_h, w_out_h, out_h,
    rate, taps, swap, order, gain, w_in, b_in, w_out,
    model, dirty, psf, rows_in, cols_in, cols_out, rows_out,
    low, low_psf, image, point, spectra, back, stepped, halves, parcel, tiles, turned,
    mixed, joined, planes, out, wide,
    load_sem, out_sem, pair_send, pair_recv, go_send, go_recv, ret_send, ret_recv, fin_send, fin_recv,
):
    row_at, col_at = lax.axis_index("rows"), lax.axis_index("cols")
    chip = row_at * 8 + col_at // 2
    core = col_at % 2
    sibling = {"rows": row_at, "cols": col_at + 1 - 2 * core}

    def at_chip(other):
        return {"rows": other // 8, "cols": (other % 8) * 2 + core}

    loads = []
    for src, dst in (
        (rows_in_h, rows_in),
        (model_h.at[0], model.at[0]),
        (psf_h, psf),
        (cols_in_h, cols_in),
        (cols_out_h, cols_out),
        (rows_out_h, rows_out),
        (dirty_h, dirty),
        (model_h.at[1], model.at[1]),
        (rate_h, rate),
        (swap_h, swap),
        (order_h, order),
        (gain_h, gain),
        (w_in_h, w_in),
        (b_in_h, b_in),
        (w_out_h, w_out),
        (taps_h, taps),
    ):
        copy = copy_here(src, dst, load_sem.at[len(loads)])
        copy.start()
        loads.append(copy)

    barrier = pltpu.get_barrier_semaphore()
    pl.semaphore_signal(barrier, inc=1, device_id=sibling, device_id_type=MESH)

    def greet(k, carry):
        pl.semaphore_signal(barrier, inc=1, device_id=at_chip(chip ^ k), device_id_type=MESH)
        return carry

    lax.fori_loop(1, CHIPS, greet, 0)

    def pair_copy(half, at):
        return pltpu.make_async_remote_copy(
            src_ref=parcel.at[half, at],
            dst_ref=halves.at[half, core, at],
            send_sem=pair_send.at[half],
            recv_sem=pair_recv.at[half],
            device_id=sibling,
            device_id_type=MESH,
        )

    def ahead(channel, at):
        blurred = dot(rows_out[at, :], back[...])
        held = model[channel, at, :].astype(F32)
        result = held + rate[channel] * (dirty[channel, at, :].astype(F32) - blurred)
        result = result.astype(BF16)
        stepped[channel, at, :] = result
        return result

    def pack(at):
        planes_at = [stepped[0, at, :].astype(F32), ahead(1, at).astype(F32)]
        planes_at = [v.reshape(8, 2, 8, IMG) for v in planes_at]
        for half in range(2):
            unit = jnp.stack([v[:, half] for v in planes_at], axis=1).reshape(128, IMG).astype(BF16)
            first = jnp.concatenate([unit[:, :128], unit[:, 256:384]], axis=1)
            second = jnp.concatenate([unit[:, 128:256], unit[:, 384:]], axis=1)
            halves[half, core, at, :] = jnp.where(core == 0, first, second)
            parcel[half, at, :] = jnp.where(core == 0, second, first)
        for half in range(2):
            pair_copy(half, at).start()

    def tile_of(planes_ref, other):
        at = pl.ds(pl.multiple_of((other // 2) * TILE, TILE), TILE)
        return planes_ref.at[:, at, pl.ds(pl.multiple_of((other % 2) * LANES, LANES), LANES)]

    def place_of(plane_ref, other):
        at = pl.ds(pl.multiple_of((other // 2) * TILE, TILE), TILE)
        return plane_ref.at[at, pl.ds(pl.multiple_of((other % 2) * 256, 256), 256)]

    core_lanes = pl.ds(pl.multiple_of(core * LANES, LANES), LANES)

    def send_tiles(channel):
        def send(k, carry):
            other = chip ^ k
            pltpu.make_async_remote_copy(
                src_ref=tile_of(halves.at[channel], other),
                dst_ref=tiles.at[channel, :, chip],
                send_sem=go_send.at[channel],
                recv_sem=go_recv.at[channel],
                device_id=at_chip(other),
                device_id_type=MESH,
            ).start()
            return carry

        lax.fori_loop(1, CHIPS, send, 0)
        copy_here(
            tile_of(halves.at[channel], chip),
            tiles.at[channel, :, chip],
            go_recv.at[channel],
        ).start()

    def return_tiles(channel):
        def send(k, carry):
            other = chip ^ k
            pltpu.make_async_remote_copy(
                src_ref=joined.at[channel, other],
                dst_ref=place_of(planes.at[channel], chip),
                send_sem=ret_send.at[channel],
                recv_sem=ret_recv.at[channel],
                device_id=at_chip(other),
                device_id_type=MESH,
            ).start()
            return carry

        lax.fori_loop(1, CHIPS, send, 0)
        copy_here(
            joined.at[channel, chip],
            place_of(planes.at[channel], chip),
            ret_recv.at[channel],
        ).start()

    def swap_mixed(channel):
        return pltpu.make_async_remote_copy(
            src_ref=mixed.at[channel],
            dst_ref=joined.at[channel, :, :, core_lanes],
            send_sem=fin_send.at[channel],
            recv_sem=fin_recv.at[channel],
            device_id=sibling,
            device_id_type=MESH,
        )

    for load in loads[:3]:
        load.wait()
    first_axis(model.at[0], psf.at[0], rows_in, image, point, low, low_psf)
    loads[3].wait()
    loads[4].wait()
    second_axis(cols_in, cols_out, image, point, spectra)
    second_axis_back(spectra, back)
    loads[5].wait()
    loads[6].wait()
    loads[8].wait()
    blocks = [pl.ds(step * 128, 128) for step in range(IMG // 128)]
    for at in blocks:
        ahead(0, at)
    loads[7].wait()
    first_axis(model.at[1], psf.at[1], rows_in, image, point, low, low_psf)
    second_axis(cols_in, cols_out, image, point, spectra)
    second_axis_back(spectra, back)
    pl.semaphore_wait(barrier, CHIPS)
    for at in blocks:
        pack(at)
    for half in range(2):
        copy_here(parcel.at[half], parcel.at[half], pair_recv.at[half]).wait()
        send_tiles(half)

    for load in loads[9:]:
        load.wait()
    w_in_t = (w_in[...].astype(F32).T * gain[...]).astype(BF16)
    w_in_t = dot(w_in_t, order[...]).astype(BF16)
    w_out_t = dot(w_out[...], order[...]).T.astype(BF16)
    bias = jnp.broadcast_to(b_in[...], (LANES, 256)).T
    bias = jnp.concatenate([bias, bias], axis=1)

    def scale_of(half):
        total = jnp.zeros((TILE, LANES), F32)
        for group in range(8):
            v = tiles[half, group // 4, pl.ds(group % 4 * 16, 16)].astype(F32)
            total = total + jnp.sum(v * v, axis=0)
        return lax.rsqrt((total[:8] + total[8:]) * (1.0 / 256) + 1e-06)

    def turn(half):
        for pair in range(4):
            sides = [
                tiles[half, pair // 2, pl.ds(pair % 2 * 32 + side * 16, 16)].reshape(256, LANES)
                for side in range(2)
            ]
            moved = dot(swap[...], jnp.concatenate(sides, axis=1)).astype(BF16)
            for side in range(2):
                for line in range(TILE):
                    channel, r = divmod(line, 8)
                    at = pl.ds(channel * 128 + pair * 32 + side * 16, 16)
                    turned[half, r // 2, at, (r % 2) * LANES : (r % 2 + 1) * LANES] = moved[
                        line * 16 : (line + 1) * 16, side * LANES : (side + 1) * LANES
                    ]

    def layers(half):
        scale = scale_of(half)
        for pair in range(4):
            factor = jnp.concatenate(
                [scale[2 * pair : 2 * pair + 1], scale[2 * pair + 1 : 2 * pair + 2]], axis=1
            )
            total = dot(w_in_t, turned[half, pair])
            hidden = jax.nn.gelu(total * factor + bias, approximate=True).astype(BF16)
            turned[half, pair] = dot(w_out_t, hidden).astype(BF16)

    def turn_back(half, which, put):
        for pair in range(2):
            sides = []
            for side in range(2):
                lines = []
                for line in range(TILE):
                    channel, r = divmod(line, 8)
                    first = channel * 128 + pair * 32 + side * 16
                    at = pl.ds(pl.multiple_of(which * CHIPS + first, 16), 16)
                    lines.append(turned[half, r // 2, at, (r % 2) * LANES : (r % 2 + 1) * LANES])
                sides.append(jnp.concatenate(lines, axis=0))
            moved = dot(swap[...], jnp.concatenate(sides, axis=1)).astype(BF16)
            for side in range(2):
                block = moved[:, side * LANES : (side + 1) * LANES].reshape(16, TILE, LANES)
                put(pl.ds(pair * 32 + side * 16, 16), block)

    def turn_back_other(half):
        def put(at, block):
            mixed[half, at] = block

        turn_back(half, 1 - core, put)
        swap_mixed(half).start()

    def turn_back_own(half):
        def put(at, block):
            joined[half, at, :, core_lanes] = block

        turn_back(half, core, put)

    for half in range(2):
        copy_here(tiles.at[half], tiles.at[half], go_recv.at[half]).wait()
        turn(half)
        layers(half)
        turn_back_other(half)
        turn_back_own(half)
        swap_mixed(half).wait_recv()
        return_tiles(half)

    zero = jnp.zeros((3, 2, BLOCKS, 8, LANES), F32)
    wide[:, :, :, :8] = zero
    wide[:, :, :, 8 + IMG :] = zero

    def own_taps(a, b, channel):
        return taps[a, b, (chip * 2 + core) * 2 + channel]

    for half in range(2):
        copy_here(planes.at[half], planes.at[half], ret_recv.at[half]).wait()
        filter_columns(planes.at[half], half, own_taps, wide)
    for channel in range(2):
        for part in range(PARTS):
            rows = pl.ds(part * (IMG // PARTS), IMG // PARTS)
            filter_rows(
                stepped.at[channel], channel, out.at[channel], wide, part * (IMG // PARTS), IMG // PARTS
            )
            copy_here(out.at[channel, rows], out_h.at[channel, rows], out_sem.at[channel, part]).start()
    for channel in range(2):
        copy_here(parcel.at[channel], parcel.at[channel], pair_send.at[channel]).wait()
        swap_mixed(channel).wait_send()
        sent = tiles.at[channel, :, pl.ds(0, CHIPS - 1)]
        copy_here(sent, sent, go_send.at[channel]).wait()
        copy_here(sent, sent, ret_send.at[channel]).wait()
        for part in range(PARTS):
            rows = pl.ds(part * (IMG // PARTS), IMG // PARTS)
            copy_here(out.at[channel, rows], out_h.at[channel, rows], out_sem.at[channel, part]).wait()


def local(model, dirty, psf, step_size, gain, w_in, b_in, w_out, kernel):
    rows_in, cols_in, cols_out, rows_out, swap, order = make_tables()
    hbm = pl.BlockSpec(memory_space=pl.ANY)
    dma = pltpu.SemaphoreType.DMA
    return pl.pallas_call(
        whole,
        out_shape=jax.ShapeDtypeStruct((2, IMG, IMG), BF16),
        in_specs=[hbm] * 15,
        out_specs=hbm,
        scratch_shapes=[
            pltpu.SMEM((2,), F32),
            pltpu.SMEM((3, 3, 256), F32),
            pltpu.VMEM((256, 256), BF16),
            pltpu.VMEM((256, 256), BF16),
            pltpu.VMEM((1, 256), F32),
            pltpu.VMEM((256, 256), BF16),
            pltpu.VMEM((1, 256), F32),
            pltpu.VMEM((256, 256), BF16),
            pltpu.VMEM((2, IMG, IMG), BF16),
            pltpu.VMEM((2, IMG, IMG), BF16),
            pltpu.VMEM((2, PSF, PSF), BF16),
            pltpu.VMEM(rows_in.shape, BF16),
            pltpu.VMEM(cols_in.shape, BF16),
            pltpu.VMEM(cols_out.shape, BF16),
            pltpu.VMEM(rows_out.shape, BF16),
            pltpu.VMEM((LEN, IMG), F32),
            pltpu.VMEM((LEN, PSF), F32),
            pltpu.VMEM((FIVE, HALF, 2 * LANES), BF16),
            pltpu.VMEM((FIVE, HALF, 2 * LANES), BF16),
            pltpu.VMEM((FIVE, HALF, 2 * LANES), F32),
            pltpu.VMEM((LEN, IMG), BF16),
            pltpu.VMEM((2, IMG, IMG), BF16),
            pltpu.VMEM((2, 2, IMG, 256), BF16),
            pltpu.VMEM((2, IMG, 256), BF16),
            pltpu.VMEM((2, 2, CHIPS, TILE, LANES), BF16),
            pltpu.VMEM((2, TILE // 4, 256, 256), BF16),
            pltpu.VMEM((2, CHIPS, TILE, LANES), BF16),
            pltpu.VMEM((2, CHIPS, TILE, 2 * LANES), BF16),
            pltpu.VMEM((2, IMG, IMG), BF16),
            pltpu.VMEM((2, IMG, IMG), BF16),
            pltpu.VMEM((3, 2, BLOCKS, IMG + 16, LANES), F32),
            dma((16,)),
        ]
        + [dma((2, PARTS))] + [dma((2,))] * 8,
        compiler_params=pltpu.CompilerParams(
            vmem_limit_bytes=64 << 20, collective_id=0, has_side_effects=True
        ),
    )(
        step_size, kernel, model, dirty, psf, rows_in, cols_in, cols_out, rows_out,
        swap, order, gain[None, :], w_in, b_in[None, :], w_out,
    )


def solution(mesh):
    split = P(("rows", "cols"), None, None)
    return jax.shard_map(
        local,
        mesh=mesh,
        in_specs=(split, split, split, P(("rows", "cols")), P(), P(), P(), P(), P()),
        out_specs=split,
        check_vma=False,
    )
```

```python
import math

import jax
import jax.numpy as jnp
import ml_dtypes
import numpy as np
from jax import lax
from jax.experimental import pallas as pl
from jax.experimental.pallas import tpu as pltpu
from jax.sharding import PartitionSpec as P

BF16 = jnp.bfloat16
F32 = jnp.float32
MESH = pl.DeviceIdType.MESH
IMG = 512
PSF = 256
LEN = IMG + PSF // 2
HALF = LEN // 2
PARTS = 4
BLOCKS = 4
TILE = 16
LANES = 128
CHIPS = 64
FIVE = LEN // LANES


def angle(freq, place):
    turns = (2.0 * freq[:, None]) * place[None, :]
    return np.mod(turns, 2 * LEN) * (math.pi / LEN)


def make_tables():
    odd = np.arange(HALF) + 0.5
    even = np.arange(LEN).astype(np.float64)
    place = np.arange(IMG).astype(np.float64)
    window = place + PSF // 2
    first = angle(odd, place)
    rows_in = np.concatenate([np.cos(first), -np.sin(first)], axis=0)
    inside = np.arange(LANES).astype(np.float64)
    cols_in, cols_out = [], []
    for shift in range(FIVE):
        second = angle(even[shift::FIVE], inside)
        cos, sin = np.cos(second.T), np.sin(second.T)
        cols_in.append(np.block([[cos, -sin], [sin, cos]]))
        cos, sin = np.cos(second), np.sin(second)
        cols_out.append(np.block([[cos, sin], [-sin, cos]]))
    cols_in, cols_out = np.stack(cols_in), np.stack(cols_out)
    last = angle(odd, window).T
    rows_out = np.concatenate([2 * np.cos(last), -2 * np.sin(last)], axis=1)
    swap = np.zeros((256, 256))
    index = np.arange(256)
    swap[index, (index % 16) * 16 + index // 16] = 1
    order = np.zeros((256, 256))
    order[index, (index % 2) * 128 + (index // 2 % 2) * CHIPS + index // 4] = 1
    tables = (rows_in, cols_in, cols_out, rows_out, swap, order)
    return [x.astype(ml_dtypes.bfloat16) for x in tables]


def dot(a, b):
    return jnp.dot(a, b, preferred_element_type=F32)


def copy_here(src, dst, sem):
    return pltpu.make_async_copy(src, dst, sem)


COS = [math.cos(2 * math.pi * k / FIVE) for k in range(FIVE)]
SIN = [math.sin(2 * math.pi * k / FIVE) for k in range(FIVE)]


def combine(zero, ones, real_even, imag_odd):
    even = [zero[p] + ones[0] * real_even[0][p] + ones[1] * real_even[1][p] for p in range(2)]
    odd = [ones[2] * imag_odd[0][p] + ones[3] * imag_odd[1][p] for p in range(2)]
    plus = (even[0] - odd[1], even[1] + odd[0])
    minus = (even[0] + odd[1], even[1] - odd[0])
    return plus, minus


def spread_five(x):
    both = [x[2][p] + x[3][p] for p in range(2)]
    apart = [x[2][p] - x[3][p] for p in range(2)]
    fourth, first = combine(x[0], (COS[1], COS[2], SIN[1], SIN[2]), (x[1], both), (x[1], apart))
    third, second = combine(x[0], (COS[2], COS[1], SIN[2], -SIN[1]), (x[1], both), (x[1], apart))
    zeroth = tuple(x[0][p] + x[1][p] + both[p] for p in range(2))
    return zeroth, first, second, third, fourth


def spread_two(x):
    out = [tuple(x[0][p] + x[1][p] for p in range(2))]
    for r in range(1, FIVE):
        out.append(
            (
                x[0][0] + COS[r] * x[1][0] + SIN[r] * x[1][1],
                x[0][1] + COS[r] * x[1][1] - SIN[r] * x[1][0],
            )
        )
    return out


def gather_five(z):
    sums = [[z[k][p] + z[FIVE - k][p] for p in range(2)] for k in (1, 2)]
    gaps = [[z[k][p] - z[FIVE - k][p] for p in range(2)] for k in (1, 2)]
    first, fourth = combine(z[0], (COS[1], COS[2], SIN[1], SIN[2]), sums, gaps)
    second, third = combine(z[0], (COS[2], COS[1], SIN[2], -SIN[1]), sums, gaps)
    return first, second, third, fourth


def lane_blocks(ref, at_re, at_im, count):
    return [
        (ref[at_re, a * LANES : (a + 1) * LANES], ref[at_im, a * LANES : (a + 1) * LANES])
        for a in range(count)
    ]


def first_axis(plane, psf, rows_in, image, point, low, low_psf):
    low_psf[...] = dot(rows_in[:, :PSF], psf[...])
    low[...] = dot(rows_in[...], plane[...])

    def rows(step, carry):
        at = pl.multiple_of(step * 16, 16)
        at_re, at_im = pl.ds(at, 16), pl.ds(HALF + at, 16)
        for ref, out, spread in ((low_psf, point, spread_two), (low, image, spread_five)):
            parts = spread(lane_blocks(ref, at_re, at_im, ref.shape[1] // LANES))
            for r in range(FIVE):
                out[r, at_re, :LANES] = parts[r][0].astype(BF16)
                out[r, at_re, LANES:] = parts[r][1].astype(BF16)
        return carry

    lax.fori_loop(0, HALF // 16, rows, 0, unroll=True)


def second_axis(cols_in, cols_out, image, point, spectra):
    for r in range(FIVE):
        x = dot(image[r], cols_in[r]) * (1.0 / (LEN * LEN))
        q = dot(point[r], cols_in[r])
        real_x, imag_x = x[:, :LANES], x[:, LANES:]
        real_q, imag_q = q[:, :LANES], q[:, LANES:]
        real_p = (real_x * real_q - imag_x * imag_q).astype(BF16)
        imag_p = (real_x * imag_q + imag_x * real_q).astype(BF16)
        spectra[r] = dot(jnp.concatenate([real_p, imag_p], axis=1), cols_out[r])


def second_axis_back(spectra, back):
    def rows(step, carry):
        at = pl.multiple_of(step * 16, 16)
        here = pl.ds(at, 16)
        z = [(spectra[r, here, :LANES], spectra[r, here, LANES:]) for r in range(FIVE)]
        for a, (re, im) in enumerate(gather_five(z)):
            back[here, a * LANES : (a + 1) * LANES] = re.astype(BF16)
            back[pl.ds(HALF + at, 16), a * LANES : (a + 1) * LANES] = im.astype(BF16)
        return carry

    lax.fori_loop(0, HALF // 16, rows, 0, unroll=True)


def filter_columns(units, half, taps, wide):
    lane = lax.broadcasted_iota(jnp.int32, (8, LANES), 1)
    zero = jnp.zeros((8, LANES), F32)
    weights = [[[taps(a, b, channel) for b in range(3)] for a in range(3)] for channel in range(2)]

    def some(step, carry):
        at = pl.multiple_of(step * 64, 64)
        v = units[pl.ds(at, 64), :].astype(F32).reshape(4, 2, 8, IMG)
        for channel in range(2):
            w = weights[channel]
            for g in range(4):
                to = pl.ds(at + g * 16 + half * 8 + 8, 8)
                m = [v[g, channel, :, j * LANES : (j + 1) * LANES] for j in range(BLOCKS)]
                left = [zero] + [pltpu.roll(x, 1, 1) for x in m]
                right = [pltpu.roll(x, LANES - 1, 1) for x in m] + [zero]
                for j in range(BLOCKS):
                    before = jnp.where(lane == 0, left[j], left[j + 1])
                    after = jnp.where(lane == LANES - 1, right[j + 1], right[j])
                    for a in range(3):
                        wide[a, channel, j, to, :] = (
                            w[a][0] * before + w[a][1] * m[j] + w[a][2] * after
                        )
        return carry

    lax.fori_loop(0, IMG // 64, some, 0, unroll=2)


def filter_rows(stepped, channel, out, wide, start, count):
    rows = 16

    def block(step, carry):
        at = pl.multiple_of(start + step * rows, rows)
        for j in range(BLOCKS):
            lines = [wide[a, channel, j, pl.ds(at + 7 + a, rows), :] for a in range(3)]
            lanes = slice(j * LANES, (j + 1) * LANES)
            total = stepped[pl.ds(at, rows), lanes].astype(F32) + (lines[0] + lines[1] + lines[2])
            out[pl.ds(at, rows), lanes] = total.astype(BF16)
        return carry

    lax.fori_loop(0, count // rows, block, 0, unroll=True)


def whole(
    rate_h, taps_h, model_h, dirty_h, psf_h, rows_in_h, cols_in_h, cols_out_h, rows_out_h,
    swap_h, order_h, gain_h, w_in_h, b_in_h, w_out_h, out_h,
    rate, taps, swap, order, gain, w_in, b_in, w_out,
    model, dirty, psf, rows_in, cols_in, cols_out, rows_out,
    low, low_psf, image, point, spectra, back, stepped, halves, parcel, tiles, turned,
    mixed, joined, planes, out, wide,
    load_sem, out_sem, pair_send, pair_recv, go_send, go_recv, ret_send, ret_recv, fin_send, fin_recv,
):
    row_at, col_at = lax.axis_index("rows"), lax.axis_index("cols")
    chip = row_at * 8 + col_at // 2
    core = col_at % 2
    sibling = {"rows": row_at, "cols": col_at + 1 - 2 * core}

    def at_chip(other):
        return {"rows": other // 8, "cols": (other % 8) * 2 + core}

    loads = []
    for src, dst in (
        (psf_h, psf),
        (rows_in_h, rows_in),
        (model_h.at[0], model.at[0]),
        (model_h.at[1], model.at[1]),
        (cols_in_h, cols_in),
        (cols_out_h, cols_out),
        (rows_out_h, rows_out),
        (dirty_h, dirty),
        (rate_h, rate),
        (swap_h, swap),
        (order_h, order),
        (gain_h, gain),
        (w_in_h, w_in),
        (b_in_h, b_in),
        (w_out_h, w_out),
        (taps_h, taps),
    ):
        copy = copy_here(src, dst, load_sem.at[len(loads)])
        copy.start()
        loads.append(copy)

    barrier = pltpu.get_barrier_semaphore()
    pl.semaphore_signal(barrier, inc=1, device_id=sibling, device_id_type=MESH)

    def greet(k, carry):
        pl.semaphore_signal(barrier, inc=1, device_id=at_chip(chip ^ k), device_id_type=MESH)
        return carry

    lax.fori_loop(1, CHIPS, greet, 0)

    def pair_copy(half, at):
        return pltpu.make_async_remote_copy(
            src_ref=parcel.at[half, at],
            dst_ref=halves.at[half, core, at],
            send_sem=pair_send.at[half],
            recv_sem=pair_recv.at[half],
            device_id=sibling,
            device_id_type=MESH,
        )

    def ahead(channel, at):
        blurred = dot(rows_out[at, :], back[channel])
        held = model[channel, at, :].astype(F32)
        result = held + rate[channel] * (dirty[channel, at, :].astype(F32) - blurred)
        result = result.astype(BF16)
        stepped[channel, at, :] = result
        return result

    def pack(at):
        planes_at = [stepped[0, at, :].astype(F32), ahead(1, at).astype(F32)]
        planes_at = [v.reshape(8, 2, 8, IMG) for v in planes_at]
        for half in range(2):
            unit = jnp.stack([v[:, half] for v in planes_at], axis=1).reshape(128, IMG).astype(BF16)
            first = jnp.concatenate([unit[:, :128], unit[:, 256:384]], axis=1)
            second = jnp.concatenate([unit[:, 128:256], unit[:, 384:]], axis=1)
            halves[half, core, at, :] = jnp.where(core == 0, first, second)
            parcel[half, at, :] = jnp.where(core == 0, second, first)
        for half in range(2):
            pair_copy(half, at).start()

    def tile_of(planes_ref, other):
        at = pl.ds(pl.multiple_of((other // 2) * TILE, TILE), TILE)
        return planes_ref.at[:, at, pl.ds(pl.multiple_of((other % 2) * LANES, LANES), LANES)]

    def place_of(plane_ref, other):
        at = pl.ds(pl.multiple_of((other // 2) * TILE, TILE), TILE)
        return plane_ref.at[at, pl.ds(pl.multiple_of((other % 2) * 256, 256), 256)]

    core_lanes = pl.ds(pl.multiple_of(core * LANES, LANES), LANES)

    def send_tiles(channel):
        def send(k, carry):
            other = chip ^ (CHIPS - k)
            pltpu.make_async_remote_copy(
                src_ref=tile_of(halves.at[channel], other),
                dst_ref=tiles.at[channel, :, chip],
                send_sem=go_send.at[channel],
                recv_sem=go_recv.at[channel],
                device_id=at_chip(other),
                device_id_type=MESH,
            ).start()
            return carry

        lax.fori_loop(1, CHIPS, send, 0)
        copy_here(
            tile_of(halves.at[channel], chip),
            tiles.at[channel, :, chip],
            go_recv.at[channel],
        ).start()

    def return_tiles(channel):
        def send(k, carry):
            other = chip ^ (CHIPS - k)
            pltpu.make_async_remote_copy(
                src_ref=joined.at[channel, other],
                dst_ref=place_of(planes.at[channel], chip),
                send_sem=ret_send.at[channel],
                recv_sem=ret_recv.at[channel],
                device_id=at_chip(other),
                device_id_type=MESH,
            ).start()
            return carry

        lax.fori_loop(1, CHIPS, send, 0)
        copy_here(
            joined.at[channel, chip],
            place_of(planes.at[channel], chip),
            ret_recv.at[channel],
        ).start()

    def swap_mixed(channel):
        return pltpu.make_async_remote_copy(
            src_ref=mixed.at[channel],
            dst_ref=joined.at[channel, :, :, core_lanes],
            send_sem=fin_send.at[channel],
            recv_sem=fin_recv.at[channel],
            device_id=sibling,
            device_id_type=MESH,
        )

    def first(channel):
        first_axis(
            model.at[channel], psf.at[channel], rows_in, image.at[channel], point.at[channel],
            low.at[channel], low_psf.at[channel],
        )

    def second(channel):
        second_axis(cols_in, cols_out, image.at[channel], point.at[channel], spectra.at[channel])

    blocks = [pl.ds(step * 128, 128) for step in range(IMG // 128)]
    for load in loads[:4]:
        load.wait()
    first(0)
    first(1)
    for load in loads[4:6]:
        load.wait()
    second(0)
    second(1)
    second_axis_back(spectra.at[0], back.at[0])
    for load in loads[6:9]:
        load.wait()
    for at in blocks:
        ahead(0, at)
    second_axis_back(spectra.at[1], back.at[1])
    pl.semaphore_wait(barrier, CHIPS)
    for at in blocks:
        pack(at)
    for half in range(2):
        copy_here(parcel.at[half], parcel.at[half], pair_recv.at[half]).wait()
        send_tiles(half)

    for load in loads[9:]:
        load.wait()
    w_in_t = (w_in[...].astype(F32).T * gain[...]).astype(BF16)
    w_in_t = dot(w_in_t, order[...]).astype(BF16)
    w_out_t = dot(w_out[...], order[...]).T.astype(BF16)
    bias = jnp.broadcast_to(b_in[...], (LANES, 256)).T
    bias = jnp.concatenate([bias, bias], axis=1)

    def scale_of(half):
        total = jnp.zeros((TILE, LANES), F32)
        for group in range(8):
            v = tiles[half, group // 4, pl.ds(group % 4 * 16, 16)].astype(F32)
            total = total + jnp.sum(v * v, axis=0)
        return lax.rsqrt((total[:8] + total[8:]) * (1.0 / 256) + 1e-06)

    def turn(half):
        for pair in range(4):
            sides = [
                tiles[half, pair // 2, pl.ds(pair % 2 * 32 + side * 16, 16)].reshape(256, LANES)
                for side in range(2)
            ]
            moved = dot(swap[...], jnp.concatenate(sides, axis=1)).astype(BF16)
            for side in range(2):
                for line in range(TILE):
                    channel, r = divmod(line, 8)
                    at = pl.ds(channel * 128 + pair * 32 + side * 16, 16)
                    turned[half, r // 2, at, (r % 2) * LANES : (r % 2 + 1) * LANES] = moved[
                        line * 16 : (line + 1) * 16, side * LANES : (side + 1) * LANES
                    ]

    def layers(half):
        scale = scale_of(half)
        for pair in range(4):
            factor = jnp.concatenate(
                [scale[2 * pair : 2 * pair + 1], scale[2 * pair + 1 : 2 * pair + 2]], axis=1
            )
            total = dot(w_in_t, turned[half, pair])
            hidden = jax.nn.gelu(total * factor + bias, approximate=True).astype(BF16)
            turned[half, pair] = dot(w_out_t, hidden).astype(BF16)

    def turn_back(half, which, put):
        for pair in range(2):
            sides = []
            for side in range(2):
                lines = []
                for line in range(TILE):
                    channel, r = divmod(line, 8)
                    first = channel * 128 + pair * 32 + side * 16
                    at = pl.ds(pl.multiple_of(which * CHIPS + first, 16), 16)
                    lines.append(turned[half, r // 2, at, (r % 2) * LANES : (r % 2 + 1) * LANES])
                sides.append(jnp.concatenate(lines, axis=0))
            moved = dot(swap[...], jnp.concatenate(sides, axis=1)).astype(BF16)
            for side in range(2):
                block = moved[:, side * LANES : (side + 1) * LANES].reshape(16, TILE, LANES)
                put(pl.ds(pair * 32 + side * 16, 16), block)

    def turn_back_other(half):
        def put(at, block):
            mixed[half, at] = block

        turn_back(half, 1 - core, put)
        swap_mixed(half).start()

    def turn_back_own(half):
        def put(at, block):
            joined[half, at, :, core_lanes] = block

        turn_back(half, core, put)

    for half in range(2):
        copy_here(tiles.at[half], tiles.at[half], go_recv.at[half]).wait()
        turn(half)
        layers(half)
        turn_back_other(half)
        turn_back_own(half)
        swap_mixed(half).wait_recv()
        return_tiles(half)

    zero = jnp.zeros((3, 2, BLOCKS, 8, LANES), F32)
    wide[:, :, :, :8] = zero
    wide[:, :, :, 8 + IMG :] = zero

    def own_taps(a, b, channel):
        return taps[a, b, (chip * 2 + core) * 2 + channel]

    for half in range(2):
        copy_here(planes.at[half], planes.at[half], ret_recv.at[half]).wait()
        filter_columns(planes.at[half], half, own_taps, wide)
    for channel in range(2):
        for part in range(PARTS):
            rows = pl.ds(part * (IMG // PARTS), IMG // PARTS)
            filter_rows(
                stepped.at[channel], channel, out.at[channel], wide, part * (IMG // PARTS), IMG // PARTS
            )
            copy_here(out.at[channel, rows], out_h.at[channel, rows], out_sem.at[channel, part]).start()
    for channel in range(2):
        copy_here(parcel.at[channel], parcel.at[channel], pair_send.at[channel]).wait()
        swap_mixed(channel).wait_send()
        sent = tiles.at[channel, :, pl.ds(0, CHIPS - 1)]
        copy_here(sent, sent, go_send.at[channel]).wait()
        copy_here(sent, sent, ret_send.at[channel]).wait()
        for part in range(PARTS):
            rows = pl.ds(part * (IMG // PARTS), IMG // PARTS)
            copy_here(out.at[channel, rows], out_h.at[channel, rows], out_sem.at[channel, part]).wait()


def local(model, dirty, psf, step_size, gain, w_in, b_in, w_out, kernel):
    rows_in, cols_in, cols_out, rows_out, swap, order = make_tables()
    hbm = pl.BlockSpec(memory_space=pl.ANY)
    dma = pltpu.SemaphoreType.DMA
    return pl.pallas_call(
        whole,
        out_shape=jax.ShapeDtypeStruct((2, IMG, IMG), BF16),
        in_specs=[hbm] * 15,
        out_specs=hbm,
        scratch_shapes=[
            pltpu.SMEM((2,), F32),
            pltpu.SMEM((3, 3, 256), F32),
            pltpu.VMEM((256, 256), BF16),
            pltpu.VMEM((256, 256), BF16),
            pltpu.VMEM((1, 256), F32),
            pltpu.VMEM((256, 256), BF16),
            pltpu.VMEM((1, 256), F32),
            pltpu.VMEM((256, 256), BF16),
            pltpu.VMEM((2, IMG, IMG), BF16),
            pltpu.VMEM((2, IMG, IMG), BF16),
            pltpu.VMEM((2, PSF, PSF), BF16),
            pltpu.VMEM(rows_in.shape, BF16),
            pltpu.VMEM(cols_in.shape, BF16),
            pltpu.VMEM(cols_out.shape, BF16),
            pltpu.VMEM(rows_out.shape, BF16),
            pltpu.VMEM((2, LEN, IMG), F32),
            pltpu.VMEM((2, LEN, PSF), F32),
            pltpu.VMEM((2, FIVE, HALF, 2 * LANES), BF16),
            pltpu.VMEM((2, FIVE, HALF, 2 * LANES), BF16),
            pltpu.VMEM((2, FIVE, HALF, 2 * LANES), F32),
            pltpu.VMEM((2, LEN, IMG), BF16),
            pltpu.VMEM((2, IMG, IMG), BF16),
            pltpu.VMEM((2, 2, IMG, 256), BF16),
            pltpu.VMEM((2, IMG, 256), BF16),
            pltpu.VMEM((2, 2, CHIPS, TILE, LANES), BF16),
            pltpu.VMEM((2, TILE // 4, 256, 256), BF16),
            pltpu.VMEM((2, CHIPS, TILE, LANES), BF16),
            pltpu.VMEM((2, CHIPS, TILE, 2 * LANES), BF16),
            pltpu.VMEM((2, IMG, IMG), BF16),
            pltpu.VMEM((2, IMG, IMG), BF16),
            pltpu.VMEM((3, 2, BLOCKS, IMG + 16, LANES), F32),
            dma((16,)),
        ]
        + [dma((2, PARTS))] + [dma((2,))] * 8,
        compiler_params=pltpu.CompilerParams(
            vmem_limit_bytes=64 << 20, collective_id=0, has_side_effects=True
        ),
    )(
        step_size, kernel, model, dirty, psf, rows_in, cols_in, cols_out, rows_out,
        swap, order, gain[None, :], w_in, b_in[None, :], w_out,
    )


def solution(mesh):
    split = P(("rows", "cols"), None, None)
    return jax.shard_map(
        local,
        mesh=mesh,
        in_specs=(split, split, split, P(("rows", "cols")), P(), P(), P(), P(), P()),
        out_specs=split,
        check_vma=False,
    )
```

```python
import math

import jax
import jax.numpy as jnp
import ml_dtypes
import numpy as np
from jax import lax
from jax.experimental import pallas as pl
from jax.experimental.pallas import tpu as pltpu
from jax.sharding import PartitionSpec as P

BF16 = jnp.bfloat16
F32 = jnp.float32
MESH = pl.DeviceIdType.MESH
IMG = 512
PSF = 256
LEN = IMG + PSF // 2
HALF = LEN // 2
PARTS = 4
BLOCKS = 4
TILE = 16
LANES = 128
CHIPS = 64
FIVE = LEN // LANES


def angle(freq, place):
    turns = (2.0 * freq[:, None]) * place[None, :]
    return np.mod(turns, 2 * LEN) * (math.pi / LEN)


def make_tables():
    odd = np.arange(HALF) + 0.5
    even = np.arange(LEN).astype(np.float64)
    place = np.arange(IMG).astype(np.float64)
    window = place + PSF // 2
    first = angle(odd, place)
    rows_in = np.concatenate([np.cos(first), -np.sin(first)], axis=0)
    inside = np.arange(LANES).astype(np.float64)
    cols_in, cols_out = [], []
    for shift in range(FIVE):
        second = angle(even[shift::FIVE], inside)
        cos, sin = np.cos(second.T), np.sin(second.T)
        cols_in.append(np.block([[cos, -sin], [sin, cos]]))
        cos, sin = np.cos(second), np.sin(second)
        cols_out.append(np.block([[cos, sin], [-sin, cos]]))
    cols_in, cols_out = np.stack(cols_in), np.stack(cols_out)
    last = angle(odd, window).T
    rows_out = np.concatenate([2 * np.cos(last), -2 * np.sin(last)], axis=1)
    swap = np.zeros((256, 256))
    index = np.arange(256)
    swap[index, (index % 16) * 16 + index // 16] = 1
    order = np.zeros((256, 256))
    order[index, (index % 2) * 128 + (index // 2 % 2) * CHIPS + index // 4] = 1
    tables = (rows_in, cols_in, cols_out, rows_out, swap, order)
    return [x.astype(ml_dtypes.bfloat16) for x in tables]


def dot(a, b):
    return jnp.dot(a, b, preferred_element_type=F32)


def copy_here(src, dst, sem):
    return pltpu.make_async_copy(src, dst, sem)


COS = [math.cos(2 * math.pi * k / FIVE) for k in range(FIVE)]
SIN = [math.sin(2 * math.pi * k / FIVE) for k in range(FIVE)]


def combine(zero, ones, real_even, imag_odd):
    even = [zero[p] + ones[0] * real_even[0][p] + ones[1] * real_even[1][p] for p in range(2)]
    odd = [ones[2] * imag_odd[0][p] + ones[3] * imag_odd[1][p] for p in range(2)]
    plus = (even[0] - odd[1], even[1] + odd[0])
    minus = (even[0] + odd[1], even[1] - odd[0])
    return plus, minus


def spread_five(x):
    both = [x[2][p] + x[3][p] for p in range(2)]
    apart = [x[2][p] - x[3][p] for p in range(2)]
    fourth, first = combine(x[0], (COS[1], COS[2], SIN[1], SIN[2]), (x[1], both), (x[1], apart))
    third, second = combine(x[0], (COS[2], COS[1], SIN[2], -SIN[1]), (x[1], both), (x[1], apart))
    zeroth = tuple(x[0][p] + x[1][p] + both[p] for p in range(2))
    return zeroth, first, second, third, fourth


def spread_two(x):
    out = [tuple(x[0][p] + x[1][p] for p in range(2))]
    for r in range(1, FIVE):
        out.append(
            (
                x[0][0] + COS[r] * x[1][0] + SIN[r] * x[1][1],
                x[0][1] + COS[r] * x[1][1] - SIN[r] * x[1][0],
            )
        )
    return out


def gather_five(z):
    sums = [[z[k][p] + z[FIVE - k][p] for p in range(2)] for k in (1, 2)]
    gaps = [[z[k][p] - z[FIVE - k][p] for p in range(2)] for k in (1, 2)]
    first, fourth = combine(z[0], (COS[1], COS[2], SIN[1], SIN[2]), sums, gaps)
    second, third = combine(z[0], (COS[2], COS[1], SIN[2], -SIN[1]), sums, gaps)
    return first, second, third, fourth


def lane_blocks(ref, at_re, at_im, count):
    return [
        (ref[at_re, a * LANES : (a + 1) * LANES], ref[at_im, a * LANES : (a + 1) * LANES])
        for a in range(count)
    ]


def first_axis(plane, psf, rows_in, image, point, low, low_psf):
    low_psf[...] = dot(rows_in[:, :PSF], psf[...])
    low[...] = dot(rows_in[...], plane[...])

    def rows(step, carry):
        at = pl.multiple_of(step * 16, 16)
        at_re, at_im = pl.ds(at, 16), pl.ds(HALF + at, 16)
        for ref, out, spread in ((low_psf, point, spread_two), (low, image, spread_five)):
            parts = spread(lane_blocks(ref, at_re, at_im, ref.shape[1] // LANES))
            for r in range(FIVE):
                out[r, at_re, :LANES] = parts[r][0].astype(BF16)
                out[r, at_re, LANES:] = parts[r][1].astype(BF16)
        return carry

    lax.fori_loop(0, HALF // 16, rows, 0, unroll=True)


def second_axis(cols_in, cols_out, image, point, spectra):
    for r in range(FIVE):
        x = dot(image[r], cols_in[r]) * (1.0 / (LEN * LEN))
        q = dot(point[r], cols_in[r])
        real_x, imag_x = x[:, :LANES], x[:, LANES:]
        real_q, imag_q = q[:, :LANES], q[:, LANES:]
        real_p = (real_x * real_q - imag_x * imag_q).astype(BF16)
        imag_p = (real_x * imag_q + imag_x * real_q).astype(BF16)
        spectra[r] = dot(jnp.concatenate([real_p, imag_p], axis=1), cols_out[r])


def second_axis_back(spectra, back):
    def rows(step, carry):
        at = pl.multiple_of(step * 16, 16)
        here = pl.ds(at, 16)
        z = [(spectra[r, here, :LANES], spectra[r, here, LANES:]) for r in range(FIVE)]
        for a, (re, im) in enumerate(gather_five(z)):
            back[here, a * LANES : (a + 1) * LANES] = re.astype(BF16)
            back[pl.ds(HALF + at, 16), a * LANES : (a + 1) * LANES] = im.astype(BF16)
        return carry

    lax.fori_loop(0, HALF // 16, rows, 0, unroll=True)


def filter_columns(units, half, taps, wide):
    lane = lax.broadcasted_iota(jnp.int32, (8, LANES), 1)
    zero = jnp.zeros((8, LANES), F32)
    weights = [[[taps(a, b, channel) for b in range(3)] for a in range(3)] for channel in range(2)]

    def some(step, carry):
        at = pl.multiple_of(step * 64, 64)
        v = units[pl.ds(at, 64), :].astype(F32).reshape(4, 2, 8, IMG)
        for channel in range(2):
            w = weights[channel]
            for g in range(4):
                to = pl.ds(at + g * 16 + half * 8 + 8, 8)
                m = [v[g, channel, :, j * LANES : (j + 1) * LANES] for j in range(BLOCKS)]
                left = [zero] + [pltpu.roll(x, 1, 1) for x in m]
                right = [pltpu.roll(x, LANES - 1, 1) for x in m] + [zero]
                for j in range(BLOCKS):
                    before = jnp.where(lane == 0, left[j], left[j + 1])
                    after = jnp.where(lane == LANES - 1, right[j + 1], right[j])
                    for a in range(3):
                        wide[a, channel, j, to, :] = (
                            w[a][0] * before + w[a][1] * m[j] + w[a][2] * after
                        )
        return carry

    lax.fori_loop(0, IMG // 64, some, 0, unroll=2)


def filter_rows(stepped, channel, out, wide, start, count):
    rows = 16

    def block(step, carry):
        at = pl.multiple_of(start + step * rows, rows)
        for j in range(BLOCKS):
            lines = [wide[a, channel, j, pl.ds(at + 7 + a, rows), :] for a in range(3)]
            lanes = slice(j * LANES, (j + 1) * LANES)
            total = stepped[pl.ds(at, rows), lanes].astype(F32) + (lines[0] + lines[1] + lines[2])
            out[pl.ds(at, rows), lanes] = total.astype(BF16)
        return carry

    lax.fori_loop(0, count // rows, block, 0, unroll=True)


def whole(
    rate_h, taps_h, model_h, dirty_h, psf_h, rows_in_h, cols_in_h, cols_out_h, rows_out_h,
    swap_h, order_h, gain_h, w_in_h, b_in_h, w_out_h, out_h,
    rate, taps, swap, order, gain, w_in, b_in, w_out,
    model, dirty, psf, rows_in, cols_in, cols_out, rows_out,
    low, low_psf, image, point, spectra, back, stepped, halves, parcel, tiles, turned,
    mixed, joined, planes, out, wide,
    load_sem, out_sem, pair_send, pair_recv, go_send, go_recv, ret_send, ret_recv, fin_send, fin_recv,
):
    row_at, col_at = lax.axis_index("rows"), lax.axis_index("cols")
    chip = row_at * 8 + col_at // 2
    core = col_at % 2
    sibling = {"rows": row_at, "cols": col_at + 1 - 2 * core}

    def at_chip(other):
        return {"rows": other // 8, "cols": (other % 8) * 2 + core}

    loads = []
    for src, dst in (
        (psf_h, psf),
        (rows_in_h, rows_in),
        (model_h.at[0], model.at[0]),
        (model_h.at[1], model.at[1]),
        (cols_in_h, cols_in),
        (cols_out_h, cols_out),
        (rows_out_h, rows_out),
        (dirty_h, dirty),
        (rate_h, rate),
        (swap_h, swap),
        (order_h, order),
        (gain_h, gain),
        (w_in_h, w_in),
        (b_in_h, b_in),
        (w_out_h, w_out),
        (taps_h, taps),
    ):
        copy = copy_here(src, dst, load_sem.at[len(loads)])
        copy.start()
        loads.append(copy)

    barrier = pltpu.get_barrier_semaphore()
    pl.semaphore_signal(barrier, inc=1, device_id=sibling, device_id_type=MESH)

    def greet(k, carry):
        pl.semaphore_signal(barrier, inc=1, device_id=at_chip(chip ^ k), device_id_type=MESH)
        return carry

    lax.fori_loop(1, CHIPS, greet, 0)

    def pair_copy(half, at):
        return pltpu.make_async_remote_copy(
            src_ref=parcel.at[half, at],
            dst_ref=halves.at[half, core, at],
            send_sem=pair_send.at[half],
            recv_sem=pair_recv.at[half],
            device_id=sibling,
            device_id_type=MESH,
        )

    def ahead(channel, at):
        blurred = dot(rows_out[at, :], back[channel])
        held = model[channel, at, :].astype(F32)
        result = held + rate[channel] * (dirty[channel, at, :].astype(F32) - blurred)
        result = result.astype(BF16)
        stepped[channel, at, :] = result
        return result

    def pack(half, at):
        v = [stepped[c, at, :].astype(F32).reshape(8, 2, 8, IMG)[:, half] for c in range(2)]
        unit = jnp.stack(v, axis=1).reshape(128, IMG).astype(BF16)
        first = jnp.concatenate([unit[:, :128], unit[:, 256:384]], axis=1)
        second = jnp.concatenate([unit[:, 128:256], unit[:, 384:]], axis=1)
        halves[half, core, at, :] = jnp.where(core == 0, first, second)
        parcel[half, at, :] = jnp.where(core == 0, second, first)
        pair_copy(half, at).start()

    def tile_of(planes_ref, other):
        at = pl.ds(pl.multiple_of((other // 2) * TILE, TILE), TILE)
        return planes_ref.at[:, at, pl.ds(pl.multiple_of((other % 2) * LANES, LANES), LANES)]

    def place_of(plane_ref, other):
        at = pl.ds(pl.multiple_of((other // 2) * TILE, TILE), TILE)
        return plane_ref.at[at, pl.ds(pl.multiple_of((other % 2) * 256, 256), 256)]

    core_lanes = pl.ds(pl.multiple_of(core * LANES, LANES), LANES)

    def send_tiles(channel):
        def send(k, carry):
            other = chip ^ (CHIPS - k)
            pltpu.make_async_remote_copy(
                src_ref=tile_of(halves.at[channel], other),
                dst_ref=tiles.at[channel, :, chip],
                send_sem=go_send.at[channel],
                recv_sem=go_recv.at[channel],
                device_id=at_chip(other),
                device_id_type=MESH,
            ).start()
            return carry

        lax.fori_loop(1, CHIPS, send, 0)
        copy_here(
            tile_of(halves.at[channel], chip),
            tiles.at[channel, :, chip],
            go_recv.at[channel],
        ).start()

    def return_tiles(channel):
        def send(k, carry):
            other = chip ^ (CHIPS - k)
            pltpu.make_async_remote_copy(
                src_ref=joined.at[channel, other],
                dst_ref=place_of(planes.at[channel], chip),
                send_sem=ret_send.at[channel],
                recv_sem=ret_recv.at[channel],
                device_id=at_chip(other),
                device_id_type=MESH,
            ).start()
            return carry

        lax.fori_loop(1, CHIPS, send, 0)
        copy_here(
            joined.at[channel, chip],
            place_of(planes.at[channel], chip),
            ret_recv.at[channel],
        ).start()

    def swap_mixed(channel):
        return pltpu.make_async_remote_copy(
            src_ref=mixed.at[channel],
            dst_ref=joined.at[channel, :, :, core_lanes],
            send_sem=fin_send.at[channel],
            recv_sem=fin_recv.at[channel],
            device_id=sibling,
            device_id_type=MESH,
        )

    def first(channel):
        first_axis(
            model.at[channel], psf.at[channel], rows_in, image.at[channel], point.at[channel],
            low.at[channel], low_psf.at[channel],
        )

    def second(channel):
        second_axis(cols_in, cols_out, image.at[channel], point.at[channel], spectra.at[channel])

    blocks = [pl.ds(step * 128, 128) for step in range(IMG // 128)]
    for load in loads[:4]:
        load.wait()
    first(0)
    first(1)
    for load in loads[4:6]:
        load.wait()
    second(0)
    second(1)
    second_axis_back(spectra.at[0], back.at[0])
    for load in loads[6:9]:
        load.wait()
    for at in blocks:
        ahead(0, at)
    second_axis_back(spectra.at[1], back.at[1])
    pl.semaphore_wait(barrier, CHIPS)
    for at in blocks:
        ahead(1, at)
        pack(0, at)
    for at in blocks:
        pack(1, at)
    for half in range(2):
        copy_here(parcel.at[half], parcel.at[half], pair_recv.at[half]).wait()
        send_tiles(half)

    for load in loads[9:]:
        load.wait()
    w_in_t = (w_in[...].astype(F32).T * gain[...]).astype(BF16)
    w_in_t = dot(w_in_t, order[...]).astype(BF16)
    w_out_t = dot(w_out[...], order[...]).T.astype(BF16)
    bias = jnp.broadcast_to(b_in[...], (LANES, 256)).T
    bias = jnp.concatenate([bias, bias], axis=1)

    def scale_of(half):
        total = jnp.zeros((TILE, LANES), F32)
        for group in range(8):
            v = tiles[half, group // 4, pl.ds(group % 4 * 16, 16)].astype(F32)
            total = total + jnp.sum(v * v, axis=0)
        return lax.rsqrt((total[:8] + total[8:]) * (1.0 / 256) + 1e-06)

    def turn(half):
        for pair in range(4):
            sides = [
                tiles[half, pair // 2, pl.ds(pair % 2 * 32 + side * 16, 16)].reshape(256, LANES)
                for side in range(2)
            ]
            moved = dot(swap[...], jnp.concatenate(sides, axis=1)).astype(BF16)
            for side in range(2):
                for line in range(TILE):
                    channel, r = divmod(line, 8)
                    at = pl.ds(channel * 128 + pair * 32 + side * 16, 16)
                    turned[half, r // 2, at, (r % 2) * LANES : (r % 2 + 1) * LANES] = moved[
                        line * 16 : (line + 1) * 16, side * LANES : (side + 1) * LANES
                    ]

    def layers(half):
        scale = scale_of(half)
        for pair in range(4):
            factor = jnp.concatenate(
                [scale[2 * pair : 2 * pair + 1], scale[2 * pair + 1 : 2 * pair + 2]], axis=1
            )
            total = dot(w_in_t, turned[half, pair])
            hidden = jax.nn.gelu(total * factor + bias, approximate=True).astype(BF16)
            turned[half, pair] = dot(w_out_t, hidden).astype(BF16)

    def turn_back(half, which, put):
        for pair in range(2):
            sides = []
            for side in range(2):
                lines = []
                for line in range(TILE):
                    channel, r = divmod(line, 8)
                    first = channel * 128 + pair * 32 + side * 16
                    at = pl.ds(pl.multiple_of(which * CHIPS + first, 16), 16)
                    lines.append(turned[half, r // 2, at, (r % 2) * LANES : (r % 2 + 1) * LANES])
                sides.append(jnp.concatenate(lines, axis=0))
            moved = dot(swap[...], jnp.concatenate(sides, axis=1)).astype(BF16)
            for side in range(2):
                block = moved[:, side * LANES : (side + 1) * LANES].reshape(16, TILE, LANES)
                put(pl.ds(pair * 32 + side * 16, 16), block)

    def turn_back_other(half):
        def put(at, block):
            mixed[half, at] = block

        turn_back(half, 1 - core, put)
        swap_mixed(half).start()

    def turn_back_own(half):
        def put(at, block):
            joined[half, at, :, core_lanes] = block

        turn_back(half, core, put)

    for half in range(2):
        copy_here(tiles.at[half], tiles.at[half], go_recv.at[half]).wait()
        turn(half)
        layers(half)
        turn_back_other(half)
        turn_back_own(half)
        swap_mixed(half).wait_recv()
        return_tiles(half)

    zero = jnp.zeros((3, 2, BLOCKS, 8, LANES), F32)
    wide[:, :, :, :8] = zero
    wide[:, :, :, 8 + IMG :] = zero

    def own_taps(a, b, channel):
        return taps[a, b, (chip * 2 + core) * 2 + channel]

    for half in range(2):
        copy_here(planes.at[half], planes.at[half], ret_recv.at[half]).wait()
        filter_columns(planes.at[half], half, own_taps, wide)
    for channel in range(2):
        for part in range(PARTS):
            rows = pl.ds(part * (IMG // PARTS), IMG // PARTS)
            filter_rows(
                stepped.at[channel], channel, out.at[channel], wide, part * (IMG // PARTS), IMG // PARTS
            )
            copy_here(out.at[channel, rows], out_h.at[channel, rows], out_sem.at[channel, part]).start()
    for channel in range(2):
        copy_here(parcel.at[channel], parcel.at[channel], pair_send.at[channel]).wait()
        swap_mixed(channel).wait_send()
        sent = tiles.at[channel, :, pl.ds(0, CHIPS - 1)]
        copy_here(sent, sent, go_send.at[channel]).wait()
        copy_here(sent, sent, ret_send.at[channel]).wait()
        for part in range(PARTS):
            rows = pl.ds(part * (IMG // PARTS), IMG // PARTS)
            copy_here(out.at[channel, rows], out_h.at[channel, rows], out_sem.at[channel, part]).wait()


def local(model, dirty, psf, step_size, gain, w_in, b_in, w_out, kernel):
    rows_in, cols_in, cols_out, rows_out, swap, order = make_tables()
    hbm = pl.BlockSpec(memory_space=pl.ANY)
    dma = pltpu.SemaphoreType.DMA
    return pl.pallas_call(
        whole,
        out_shape=jax.ShapeDtypeStruct((2, IMG, IMG), BF16),
        in_specs=[hbm] * 15,
        out_specs=hbm,
        scratch_shapes=[
            pltpu.SMEM((2,), F32),
            pltpu.SMEM((3, 3, 256), F32),
            pltpu.VMEM((256, 256), BF16),
            pltpu.VMEM((256, 256), BF16),
            pltpu.VMEM((1, 256), F32),
            pltpu.VMEM((256, 256), BF16),
            pltpu.VMEM((1, 256), F32),
            pltpu.VMEM((256, 256), BF16),
            pltpu.VMEM((2, IMG, IMG), BF16),
            pltpu.VMEM((2, IMG, IMG), BF16),
            pltpu.VMEM((2, PSF, PSF), BF16),
            pltpu.VMEM(rows_in.shape, BF16),
            pltpu.VMEM(cols_in.shape, BF16),
            pltpu.VMEM(cols_out.shape, BF16),
            pltpu.VMEM(rows_out.shape, BF16),
            pltpu.VMEM((2, LEN, IMG), F32),
            pltpu.VMEM((2, LEN, PSF), F32),
            pltpu.VMEM((2, FIVE, HALF, 2 * LANES), BF16),
            pltpu.VMEM((2, FIVE, HALF, 2 * LANES), BF16),
            pltpu.VMEM((2, FIVE, HALF, 2 * LANES), F32),
            pltpu.VMEM((2, LEN, IMG), BF16),
            pltpu.VMEM((2, IMG, IMG), BF16),
            pltpu.VMEM((2, 2, IMG, 256), BF16),
            pltpu.VMEM((2, IMG, 256), BF16),
            pltpu.VMEM((2, 2, CHIPS, TILE, LANES), BF16),
            pltpu.VMEM((2, TILE // 4, 256, 256), BF16),
            pltpu.VMEM((2, CHIPS, TILE, LANES), BF16),
            pltpu.VMEM((2, CHIPS, TILE, 2 * LANES), BF16),
            pltpu.VMEM((2, IMG, IMG), BF16),
            pltpu.VMEM((2, IMG, IMG), BF16),
            pltpu.VMEM((3, 2, BLOCKS, IMG + 16, LANES), F32),
            dma((16,)),
        ]
        + [dma((2, PARTS))] + [dma((2,))] * 8,
        compiler_params=pltpu.CompilerParams(
            vmem_limit_bytes=64 << 20, collective_id=0, has_side_effects=True
        ),
    )(
        step_size, kernel, model, dirty, psf, rows_in, cols_in, cols_out, rows_out,
        swap, order, gain[None, :], w_in, b_in[None, :], w_out,
    )


def solution(mesh):
    split = P(("rows", "cols"), None, None)
    return jax.shard_map(
        local,
        mesh=mesh,
        in_specs=(split, split, split, P(("rows", "cols")), P(), P(), P(), P(), P()),
        out_specs=split,
        check_vma=False,
    )
```
